256 devices in a mesh: gy: 16 (over y, z_lo, core), gz: 16 (over x, z_hi).
Axes of the slice: x: 4, y: 4, z: 8 (z_hi: 4, z_lo: 2; z = z_hi * 2 + z_lo), core: 2. Of those that a mesh axis runs over, the one named last changes fastest.
Arguments:
- velocity: float32 [3, 16, 1536, 1536], P(None, None, 'gy', 'gz'), may hold values from -6 to 6
- vorticity: float32 [3, 16, 1536, 1536], P(None, None, 'gy', 'gz'), may hold values from -6 to 6
- q_state: float32 [2, 3, 16, 768, 1536], P(None, None, 'gz', 'gy'), may hold values from -6 to 6
- u_state: float32 [2, 3, 16, 768, 1536], P(None, None, 'gz', 'gy'), may hold values from -6 to 6
- shift: int32 [16], P('gz'), may hold values from 0 to 1535
- requests: int32 [16, 16, 16, 4], P('gy', 'gz'), may hold values from 0 to 191, as said below
- tracer_slot: int32 [16, 16, 16, 32], P('gy', 'gz'), may hold values from 0 to 3
- tracer_row: int32 [16, 16, 16, 32], P('gy', 'gz'), may hold values from 0 to 6
- tracer_col: int32 [16, 16, 16, 32], P('gy', 'gz'), may hold values from 0 to 94
- tracer_count: int32 [16, 16, 16], P('gy', 'gz'), may hold values from 1 to 32
- tracer_frac: float32 [2, 16, 16, 16, 32], P(None, 'gy', 'gz'), may hold values from 0 to 1
- tracer_vel: float32 [3, 16, 16, 16, 32], P(None, 'gy', 'gz'), may hold values from -6 to 6
Outputs:
- q_next: float32 [2, 3, 16, 768, 1536], P(None, None, 'gz', 'gy')
- u_next: float32 [2, 3, 16, 768, 1536], P(None, None, 'gz', 'gy')
- tracer_next: float32 [3, 16, 16, 16, 32], P(None, 'gy', 'gz')
The draws below stay inside these ranges and needn't reach their ends.
Inputs may be any that keep to these rules, and one draw needn't show every extreme that they name: `requests`: within one owner and holder the 4 requested blocks are different blocks of that holder.
All inputs are finite; a program needn't handle non-finite values.
Results may differ from the reference program's by a relative error of at most 0.003.
Values may be sent and summed in bfloat16 or wider, within the bound.
A program may use at most 192 MiB of HBM per device.

```python
import math
import jax
import jax.numpy as jnp
from jax import lax

NY = 1536
NZ = 1536
BR = 8
CAP = 4
TPP = 32
X = 16
YL = 96
ZL = 96
KZ = 768
RB = 12
NB = 192
N_GY = 16
N_GZ = 16


def draw_requests(key, part):
    key = jax.random.fold_in(key, 11)
    keys = jax.random.split(key, N_GY * N_GZ * N_GZ)
    chosen = jax.vmap(lambda single: jax.random.permutation(single, NB)[:CAP])(keys)
    return chosen.reshape(N_GY, N_GZ, N_GZ, CAP).astype(jnp.int32)


def draw_tracer_count(key, part):
    key = jax.random.fold_in(key, 23)
    first_key, second_key, third_key = jax.random.split(key, 3)
    counts = jax.random.randint(first_key, (N_GY, N_GZ, N_GZ), TPP // 3, TPP + 1)
    divisor = jax.random.randint(second_key, (N_GY, 1, N_GZ), 1, 3)
    counts = jnp.maximum(counts // divisor, 1).reshape(-1)
    spot = jax.random.randint(third_key, (), 0, N_GY * N_GZ * N_GZ)
    counts = counts.at[spot].set(TPP)
    return counts.reshape(N_GY, N_GZ, N_GZ).astype(jnp.int32)


def touch_ends(array, rng, smallest, largest):
    index_at = [jax.random.randint(jax.random.fold_in(rng, axis), (), 0, length) for axis, length in enumerate(array.shape)]
    widest = array.shape.index(max(array.shape))
    beside = index_at[:widest] + [(index_at[widest] + 1) % array.shape[widest]] + index_at[widest + 1:]
    return array.at[tuple(index_at)].set(smallest).at[tuple(beside)].set(largest)


def block_scale(rng, dims, shards, smallest, largest):
    loudness = 1.0
    for axis_at, blocks in shards:
        steps = jax.random.uniform(jax.random.fold_in(jax.random.fold_in(rng, 6), axis_at), (blocks,), jnp.float32, smallest / len(shards), largest / len(shards))
        loudness = loudness * jnp.repeat(jnp.exp(steps), dims[axis_at] // blocks).reshape((-1,) + (1,) * (len(dims) - 1 - axis_at))
    return loudness


def centred(key, extent, spread, limit, cuts=(), held_as=jnp.bfloat16):
    loudness = block_scale(key, extent, cuts, -0.22, 0.18) if cuts else 1.0
    values = jax.random.normal(key, extent, jnp.float32) * spread * loudness
    return jnp.minimum(jnp.maximum(values, -limit), limit).astype(held_as)


def setup_inputs(seed: int = 0) -> dict:
    arg_keys = jax.random.split(jax.random.key(seed), 13)
    velocity = centred(arg_keys[0], (3, X, NY, NZ), 1.0, 6.0, ((2, 16), (3, 16)), jnp.float32)
    vorticity = centred(arg_keys[1], (3, X, NY, NZ), 1.0, 6.0, ((2, 16), (3, 16)), jnp.float32)
    q_state = centred(arg_keys[2], (2, 3, X, KZ, NY), 1.0, 6.0, ((2, 16), (3, 16)), jnp.float32)
    u_state = centred(arg_keys[3], (2, 3, X, KZ, NY), 1.0, 6.0, ((2, 16), (3, 16)), jnp.float32)
    shift = touch_ends(jax.random.randint(arg_keys[4], (X,), 0, NY), jax.random.fold_in(arg_keys[4], 1), 0, NY - 1).astype(jnp.int32)
    requests = draw_requests(jax.random.fold_in(arg_keys[12], 71), 0)
    tracer_slot = touch_ends(jax.random.randint(arg_keys[6], (N_GY, N_GZ, N_GZ, TPP), 0, CAP), jax.random.fold_in(arg_keys[6], 1), 0, CAP - 1).astype(jnp.int32)
    tracer_row = touch_ends(jax.random.randint(arg_keys[7], (N_GY, N_GZ, N_GZ, TPP), 0, BR - 1), jax.random.fold_in(arg_keys[7], 1), 0, (BR - 1) - 1).astype(jnp.int32)
    tracer_col = touch_ends(jax.random.randint(arg_keys[8], (N_GY, N_GZ, N_GZ, TPP), 0, ZL - 1), jax.random.fold_in(arg_keys[8], 1), 0, (ZL - 1) - 1).astype(jnp.int32)
    tracer_count = draw_tracer_count(jax.random.fold_in(arg_keys[12], 71), 0)
    tracer_frac = jnp.clip(1.0 * jax.random.uniform(arg_keys[10], (2, N_GY, N_GZ, N_GZ, TPP), jnp.float32) ** block_scale(arg_keys[10], (2, N_GY, N_GZ, N_GZ, TPP), ((1, 16), (2, 16)), -0.2, 0.2), 0.0, 1.0)
    tracer_vel = centred(arg_keys[11], (3, N_GY, N_GZ, N_GZ, TPP), 1.0, 6.0, ((1, 16), (2, 16)), jnp.float32)
    return dict(velocity=velocity, vorticity=vorticity, q_state=q_state, u_state=u_state, shift=shift, requests=requests, tracer_slot=tracer_slot, tracer_row=tracer_row, tracer_col=tracer_col, tracer_count=tracer_count, tracer_frac=tracer_frac, tracer_vel=tracer_vel)


stencil_steps = ((0, 0), (0, 1), (1, 0), (1, 1))
drag_mass = 24.0
relax_ratio = 0.5
coef_keep = -5.0 / 9.0
coef_add = 15.0 / 16.0
time_step = 0.5

def stencil_weights(fraction):
    along_y = fraction[0]
    along_z = fraction[1]
    return [(1.0 - along_y) * (1.0 - along_z), (1.0 - along_y) * along_z, along_y * (1.0 - along_z), along_y * along_z]

def dft_tables(length, modes):
    row_index = lax.broadcasted_iota(jnp.int32, (length, modes), 0)
    col_index = lax.broadcasted_iota(jnp.int32, (length, modes), 1)
    phase = (row_index * col_index % length).astype(jnp.float32) * (2.0 * math.pi / length)
    return (jnp.cos(phase).astype(jnp.bfloat16), jnp.sin(phase).astype(jnp.bfloat16))

def cross_product(first, second):
    return jnp.stack([first[1] * second[2] - first[2] * second[1], first[2] * second[0] - first[0] * second[2], first[0] * second[1] - first[1] * second[0]])

def spectral_update(parts, q_state, u_state, kz_values, ny_len, nz_len):
    ky_index = jnp.arange(ny_len, dtype=jnp.int32)
    ky_values = jnp.where(ky_index < ny_len // 2, ky_index, ky_index - ny_len).astype(jnp.float32)
    kz_column = kz_values[:, None]
    wave_square = kz_column * kz_column + ky_values * ky_values
    inverse = 1.0 / jnp.maximum(wave_square, 1.0)
    damping = jnp.exp(-2.0 * wave_square / (ny_len * nz_len))
    projected = []
    for spectrum in parts:
        radial = ky_values * spectrum[1] + kz_column * spectrum[2]
        projected.append(jnp.stack([spectrum[0], spectrum[1] - ky_values * radial * inverse, spectrum[2] - kz_column * radial * inverse]))
    stacked = jnp.stack(projected)
    q_next = coef_keep * q_state + time_step * damping * stacked
    return (q_next, u_state + coef_add * q_next)

def contract_y(left, table):
    return jnp.einsum('cxyk,yl->cxkl', left.astype(jnp.float32), table.astype(jnp.float32), precision=lax.Precision.HIGHEST)

def reference(velocity, vorticity, q_state, u_state, shift, requests, tracer_slot, tracer_row, tracer_col, tracer_count, tracer_frac, tracer_vel):
    vel_bf = velocity.astype(jnp.bfloat16)
    tracer_shape = tracer_slot.shape
    gy_rank = lax.broadcasted_iota(jnp.int32, tracer_shape, 0)
    peer_rank = lax.broadcasted_iota(jnp.int32, tracer_shape, 2)
    position = lax.broadcasted_iota(jnp.int32, tracer_shape, 3)
    block_ids = jnp.take_along_axis(requests, tracer_slot, axis=3)
    plane_ids = block_ids // RB
    first_y = gy_rank * YL + block_ids % RB * BR + tracer_row
    first_z = peer_rank * ZL + tracer_col
    weights = stencil_weights(tracer_frac)
    at_tracer = jnp.zeros(tracer_vel.shape, jnp.float32)
    for number in range(4):
        step_y, step_z = stencil_steps[number]
        sample = vel_bf[:, plane_ids, first_y + step_y, first_z + step_z].astype(jnp.float32)
        at_tracer = at_tracer + weights[number] * sample
    alive = (position < tracer_count[..., None]).astype(jnp.float32)
    tracer_next = tracer_vel + relax_ratio * alive * (at_tracer - tracer_vel)
    drag = drag_mass * alive * (tracer_vel - at_tracer)
    feedback = jnp.zeros(velocity.shape, jnp.float32)
    for number in range(4):
        step_y, step_z = stencil_steps[number]
        feedback = feedback.at[:, plane_ids, first_y + step_y, first_z + step_z].add(weights[number] * drag)
    forcing = (cross_product(velocity, vorticity) + feedback).astype(jnp.bfloat16)
    cos_z, sin_z = dft_tables(NZ, KZ)
    wide = forcing.astype(jnp.float32)
    z_real = jnp.einsum('cxyz,zk->cxyk', wide, cos_z.astype(jnp.float32), precision=lax.Precision.HIGHEST).astype(jnp.bfloat16)
    z_imag = (-jnp.einsum('cxyz,zk->cxyk', wide, sin_z.astype(jnp.float32), precision=lax.Precision.HIGHEST)).astype(jnp.bfloat16)
    cos_y, sin_y = dft_tables(NY, NY)
    scale = 1.0 / math.sqrt(NY * NZ)
    h_real = (contract_y(z_real, cos_y) + contract_y(z_imag, sin_y)) * scale
    h_imag = (contract_y(z_imag, cos_y) - contract_y(z_real, sin_y)) * scale
    shifted = (jnp.arange(NY, dtype=jnp.int32)[None, :] - shift[:, None]) % NY
    h_real = jnp.take_along_axis(h_real, shifted[None, :, None, :], axis=3)
    h_imag = jnp.take_along_axis(h_imag, shifted[None, :, None, :], axis=3)
    kz_values = jnp.arange(KZ, dtype=jnp.int32).astype(jnp.float32)
    q_next, u_next = spectral_update((h_real, h_imag), q_state, u_state, kz_values, NY, NZ)
    return (q_next, u_next, tracer_next)
```

```python
import functools
import math

import jax
import jax.numpy as jnp
import ml_dtypes
import numpy as np
from jax import lax
from jax.experimental import pallas as pl
from jax.experimental.pallas import tpu as pltpu
from jax.sharding import PartitionSpec as P

MESH = pl.DeviceIdType.MESH
BF16 = jnp.bfloat16
F32 = jnp.float32

NY = 1536
NZ = 1536
DEV = 16
LOC = 96
PLANES = 16
KZL = 48
TPP = 32
TR = DEV * TPP
MAIN = 216
PIECE = 224
QUARTER = 24
WIDE = PIECE + 80

drag_mass = 24.0
relax_ratio = 0.5
coef_keep = -5.0 / 9.0
coef_add = 15.0 / 16.0
time_step = 0.5


def dft_base(length):
    index = np.arange(length, dtype=np.int64)
    phase = (np.outer(index, index) % length).astype(np.float32) * np.float32(2.0 * math.pi / length)
    return np.cos(phase).astype(ml_dtypes.bfloat16), np.sin(phase).astype(ml_dtypes.bfloat16)


@functools.lru_cache(maxsize=None)
def tables():
    cos, sin = dft_base(NY)
    first = np.zeros((DEV, 128, DEV, 128), ml_dtypes.bfloat16)
    kz_cos = cos[:, : NZ // 2].reshape(DEV, LOC, DEV, KZL)
    kz_sin = sin[:, : NZ // 2].reshape(DEV, LOC, DEV, KZL)
    first[:, :LOC, :, :KZL] = kz_cos
    first[:, :LOC, :, KZL : 2 * KZL] = -kz_sin
    place = np.arange(NY)
    row_of = (place % 384) // QUARTER * LOC + (place // 384) * QUARTER + place % QUARTER
    second = np.concatenate([cos[row_of], sin[row_of]], axis=0)
    return first.reshape(DEV * 128, DEV * 128), second


def lane_index(shape):
    return lax.broadcasted_iota(jnp.int32, shape, len(shape) - 1)


def pack(main, last):
    lane = lane_index((QUARTER, 128))
    out = []
    for comp in range(3):
        low = last[comp * QUARTER : (comp + 1) * QUARTER]
        for third in range(3):
            at = comp * 72 + third * QUARTER
            turned = pltpu.roll(low, 96 - 32 * third, 1)
            out.append(jnp.where(lane < LOC, main[at : at + QUARTER], turned))
    out.append(jnp.zeros((8, 128), F32))
    return jnp.concatenate(out, axis=0)


def unpack_last(piece):
    lane = lane_index((QUARTER, 128))
    out = []
    for comp in range(3):
        parts = [
            pltpu.roll(piece[comp * 72 + third * QUARTER : comp * 72 + (third + 1) * QUARTER], (32 * third + 32) % 128, 1)
            for third in range(3)
        ]
        out.append(
            jnp.where(lane < 32, parts[0], jnp.where(lane < 64, parts[1], jnp.where(lane < LOC, parts[2], 0.0)))
        )
    out.append(jnp.zeros((8, 128), F32))
    return jnp.concatenate(out, axis=0)


def widen(block):
    return jnp.concatenate([block, jnp.zeros((block.shape[0], 128 - block.shape[1]), block.dtype)], axis=1)


def exchange_kernel(
    vel_hbm,
    vort_hbm,
    first_hbm,
    second_hbm,
    requests_ref,
    slot_ref,
    row_ref,
    col_ref,
    count_ref,
    frac_ref,
    tvel_ref,
    spec_hbm,
    at_ref,
    vel,
    vort,
    first,
    second,
    vel_b,
    hot,
    picked,
    spread,
    fields,
    row_lanes,
    at_cols,
    t_send,
    t_recv,
    a_send,
    a_recv,
    send1,
    recv1,
    send2,
    recv2,
    left,
    spec,
    load_sem,
    own_sem,
    out_sem,
    t_ssem,
    t_rsem,
    a_ssem,
    a_rsem,
    ssem1,
    rsem1,
    ssem2,
    rsem2,
):
    gy = lax.axis_index("gy")
    gz = lax.axis_index("gz")
    my_x, my_h = gz // 4, lax.rem(gz, 4)

    def along(base, step):
        return lax.rem(base + step, DEV)

    barrier = pltpu.get_barrier_semaphore()
    for step in range(1, DEV):
        pl.semaphore_signal(barrier, inc=1, device_id=(gy, along(gz, step)), device_id_type=MESH)
    for step in range(1, DEV):
        pl.semaphore_signal(barrier, inc=1, device_id=(along(gy, step), gz), device_id_type=MESH)
    loads = [
        pltpu.make_async_copy(vel_hbm, vel, load_sem.at[0]),
        pltpu.make_async_copy(vort_hbm, vort, load_sem.at[1]),
        pltpu.make_async_copy(first_hbm, first, load_sem.at[2]),
        pltpu.make_async_copy(second_hbm, second, load_sem.at[3]),
    ]
    for load in loads:
        load.start()

    slots = slot_ref[...]
    wanted = requests_ref[...]
    block = jnp.zeros((DEV, TPP), jnp.int32)
    for number in range(4):
        block = jnp.where(slots == number, wanted[:, number : number + 1], block)
    counts = jnp.broadcast_to(count_ref[...], (DEV, DEV))
    diagonal = lax.broadcasted_iota(jnp.int32, (DEV, DEV), 0) == lax.broadcasted_iota(jnp.int32, (DEV, DEV), 1)
    count_col = jnp.sum(jnp.where(diagonal, counts, 0).astype(F32), axis=1, keepdims=True)
    alive = (lane_index((DEV, TPP)).astype(F32) < count_col).astype(F32)
    listed = [
        (block * 8 + row_ref[...]).astype(F32),
        col_ref[...].astype(F32),
        frac_ref[0],
        frac_ref[1],
        tvel_ref[0],
        tvel_ref[1],
        tvel_ref[2],
        alive,
    ]
    t_send[...] = jnp.zeros(t_send.shape, F32)
    for peer in range(DEV):
        for number in range(8):
            t_send[peer, number : number + 1, 0:TPP] = listed[number][peer : peer + 1]

    pl.semaphore_wait(barrier, 2 * (DEV - 1))

    def to_holder(step):
        peer = along(gz, step)
        return pltpu.make_async_remote_copy(
            src_ref=t_send.at[peer],
            dst_ref=t_recv.at[gz],
            send_sem=t_ssem.at[step],
            recv_sem=t_rsem.at[step],
            device_id=(gy, peer),
            device_id_type=MESH,
        )

    for step in range(1, DEV):
        to_holder(step).start()
    own = pltpu.make_async_copy(t_send.at[gz], t_recv.at[gz], own_sem.at[0])
    own.start()

    loads[0].wait()
    for comp in range(3):
        @pl.loop(0, PLANES)
        def _(plane):
            rows = pl.ds(pl.multiple_of(plane * LOC, LOC), LOC)
            vel_b[rows, comp * 128 : (comp + 1) * 128] = widen(vel[comp, plane]).astype(BF16)

    own.wait()
    for step in range(1, DEV):
        to_holder(step).wait()

    arrived = t_recv[...]
    turned = arrived.reshape(128, 128).T
    for owner in range(DEV):
        fields[owner * TPP : (owner + 1) * TPP, :] = pltpu.roll(turned[0:TPP], (128 - owner * 8) % 128, 1)
    lane_row = lane_index((1, 128))
    for quad in range(4):
        total = jnp.zeros((1, 128), F32)
        for number in range(4):
            total = jnp.where(
                lane_row // TPP == number,
                pltpu.roll(arrived[quad * 4 + number, 0:1], number * TPP, 1),
                total,
            )
        row_lanes[0:1, quad * 128 : (quad + 1) * 128] = total

    @pl.loop(0, TR // 32)
    def _(part):
        rows = pl.ds(pl.multiple_of(part * 32, 32), 32)
        lower = pl.ds(pl.multiple_of(part * 32 + TR, 32), 32)
        start = fields[rows, 0:1]
        cell_row = lane_index((32, PLANES * LOC)).astype(F32)
        hot[rows, :] = jnp.where(cell_row == start, 1.0, 0.0).astype(BF16)
        hot[lower, :] = jnp.where(cell_row == start + 1.0, 1.0, 0.0).astype(BF16)

    @pl.loop(0, 2 * TR // 256)
    def _(part):
        rows = pl.ds(pl.multiple_of(part * 256, 256), 256)
        picked[rows, :] = jnp.dot(hot[rows, :], vel_b[...], preferred_element_type=F32)

    @pl.loop(0, TR // 32)
    def _(part):
        rows = pl.ds(pl.multiple_of(part * 32, 32), 32)
        lower = pl.ds(pl.multiple_of(part * 32 + TR, 32), 32)
        table = fields[rows, :]
        along_y, along_z = table[:, 2:3], table[:, 3:4]
        lane = lane_index((32, 128)).astype(F32)
        start = table[:, 1:2]
        cell = jnp.where(lane == start, 1.0 - along_z, jnp.where(lane == start + 1.0, along_z, 0.0))
        upper_w = (1.0 - along_y) * cell
        lower_w = along_y * cell
        ats = jnp.zeros((32, 128), F32)
        lane_i = lane_index((32, 128))
        for comp in range(3):
            cols = slice(comp * 128, (comp + 1) * 128)
            at = jnp.sum(upper_w * picked[rows, cols] + lower_w * picked[lower, cols], axis=1, keepdims=True)
            ats = jnp.where(lane_i == comp, at, ats)
            drag = drag_mass * table[:, 7:8] * (table[:, 4 + comp : 5 + comp] - at)
            for weight, place in ((upper_w, rows), (lower_w, lower)):
                value = weight * drag
                high = value.astype(BF16)
                spread[place, comp * 256 : comp * 256 + 128] = high
                spread[place, comp * 256 + 128 : (comp + 1) * 256] = (value - high.astype(F32)).astype(BF16)
        at_cols[rows, :] = ats

    loads[1].wait()
    order = [(dx, dh) for dh in (2, 1, 3, 0) for dx in (2, 1, 3, 0)]

    def target(dx, dh):
        return lax.rem(my_x + dx, 4) * 4 + lax.rem(my_h + dh, 4)

    def of_step(step):
        quarter, third = step // 4, lax.rem(step, 4)
        far = lambda n: jnp.where(n == 0, 2, jnp.where(n == 1, 1, jnp.where(n == 2, 3, 0)))
        return far(third), far(quarter)

    def to_plane(step):
        dx, dh = of_step(step)
        peer = target(dx, dh)
        return pltpu.make_async_remote_copy(
            src_ref=send1.at[peer],
            dst_ref=recv1.at[pl.ds(0, PIECE), pl.ds(pl.multiple_of(gz * 128, 128), 128)],
            send_sem=ssem1.at[step],
            recv_sem=rsem1.at[step],
            device_id=(gy, peer),
            device_id_type=MESH,
        )

    def make_plane(plane):
        base = plane * LOC
        cell_row = (lax.broadcasted_iota(jnp.int32, (LOC, TR), 0) + base).astype(F32)
        starts = row_lanes[0:1, :]
        upper = jnp.where(cell_row == starts, 1.0, 0.0).astype(BF16)
        lower = jnp.where(cell_row == starts + 1.0, 1.0, 0.0).astype(BF16)
        both = jnp.concatenate([upper, lower], axis=1)
        u = [widen(vel[comp, plane]) for comp in range(3)]
        w = [widen(vort[comp, plane]) for comp in range(3)]
        mains, lasts = [], []
        for comp in range(3):
            a, b = (comp + 1) % 3, (comp + 2) % 3
            fed = jnp.dot(both, spread[:, comp * 256 : (comp + 1) * 256], preferred_element_type=F32)
            force = (u[a] * w[b] - u[b] * w[a]) + (fed[:, 0:128] + fed[:, 128:256])
            mains.append(force[0:72])
            lasts.append(force[72:96])
        send1[plane] = pack(jnp.concatenate(mains, axis=0), jnp.concatenate(lasts, axis=0)).astype(BF16)

    @pl.loop(0, DEV - 1)
    def _(step):
        dx, dh = of_step(step)
        make_plane(target(dx, dh))
        to_plane(step).start()

    make_plane(gz)
    own1 = pltpu.make_async_copy(
        send1.at[gz], recv1.at[pl.ds(0, PIECE), pl.ds(pl.multiple_of(gz * 128, 128), 128)], own_sem.at[1]
    )
    own1.start()

    total = jnp.zeros((TPP, 128), F32)
    lane_i = lane_index((TPP, 128))
    for owner in range(DEV):
        moved = pltpu.roll(at_cols[owner * TPP : (owner + 1) * TPP, :], owner * 8, 1)
        total = jnp.where(lane_i // 8 == owner, moved, total)
    back = jnp.concatenate([total, jnp.zeros((128 - TPP, 128), F32)], axis=0).T
    a_send[...] = back.reshape(DEV, 8, 128)

    def to_owner(step):
        peer = along(gz, step)
        return pltpu.make_async_remote_copy(
            src_ref=a_send.at[peer],
            dst_ref=a_recv.at[gz],
            send_sem=a_ssem.at[step],
            recv_sem=a_rsem.at[step],
            device_id=(gy, peer),
            device_id_type=MESH,
        )

    for step in range(1, DEV):
        to_owner(step).start()
    own2 = pltpu.make_async_copy(a_send.at[gz], a_recv.at[gz], own_sem.at[2])
    own2.start()

    own1.wait()

    @pl.loop(0, DEV - 1)
    def _(step):
        to_plane(step).wait()

    @pl.loop(0, DEV)
    def _(source):
        cols = pl.ds(pl.multiple_of(source * 128, 128), 128)
        piece = recv1[0:PIECE, cols].astype(F32)
        recv1[PIECE:WIDE, cols] = unpack_last(piece).astype(BF16)

    loads[2].wait()

    def to_owner_kz(step):
        peer = lax.rem(gy // 2 + step // 2, 8) * 2 + lax.rem(gy + step, 2)
        return pltpu.make_async_remote_copy(
            src_ref=send2.at[peer],
            dst_ref=recv2.at[gy],
            send_sem=ssem2.at[step],
            recv_sem=rsem2.at[step],
            device_id=(peer, gz),
            device_id_type=MESH,
        )

    def make_pair(turn):
        pair = lax.rem(gy // 2 + turn, 8)
        cols = pl.ds(pl.multiple_of(pair * 256, 256), 256)
        out = jnp.dot(recv1[...], first[:, cols], preferred_element_type=F32)
        for half in range(2):
            lanes = slice(half * 128, (half + 1) * 128)
            send2[pair * 2 + half] = pack(out[0:MAIN, lanes], out[PIECE : PIECE + 72, lanes]).astype(BF16)

    @pl.loop(1, 8)
    def _(turn):
        make_pair(turn)
        to_owner_kz(2 * turn).start()
        to_owner_kz(2 * turn + 1).start()

    make_pair(0)
    to_owner_kz(1).start()
    own3 = pltpu.make_async_copy(send2.at[gy], recv2.at[gy], own_sem.at[3])
    own3.start()

    own2.wait()
    for step in range(1, DEV):
        to_owner(step).wait()
    at_ref[...] = a_recv[...]

    own3.wait()

    @pl.loop(1, DEV)
    def _(step):
        to_owner_kz(step).wait()

    for comp in range(3):
        for third in range(3):
            at = comp * 72 + third * QUARTER
            stacked = recv2[:, 0:PIECE, :].astype(F32)[:, at : at + QUARTER].reshape(DEV * QUARTER, 128)
            for part in range(3):
                tile = stacked[part * 128 : (part + 1) * 128].T
                cols = slice(third * 384 + part * 128, third * 384 + (part + 1) * 128)
                real, imag = tile[0:KZL].astype(BF16), tile[KZL : 2 * KZL].astype(BF16)
                rows_re = slice(comp * KZL, (comp + 1) * KZL)
                rows_im = slice((3 + comp) * KZL, (4 + comp) * KZL)
                more = slice(NY + cols.start, NY + cols.stop)
                left[rows_re, cols] = real
                left[rows_re, more] = imag
                left[rows_im, cols] = imag
                left[rows_im, more] = -real
                last_cols = slice(1152 + part * 128, 1152 + (part + 1) * 128)
                last_more = slice(NY + last_cols.start, NY + last_cols.stop)
                for piece in range(2):
                    lo = third * 32 + piece * 16
                    value = tile[96 + piece * 16 : 112 + piece * 16].astype(BF16)
                    if lo < KZL:
                        left[comp * KZL + lo : comp * KZL + lo + 16, last_cols] = value
                        left[(3 + comp) * KZL + lo : (3 + comp) * KZL + lo + 16, last_more] = -value
                    else:
                        lo -= KZL
                        left[comp * KZL + lo : comp * KZL + lo + 16, last_more] = value
                        left[(3 + comp) * KZL + lo : (3 + comp) * KZL + lo + 16, last_cols] = value

    loads[3].wait()

    def write(tile):
        cols = pl.ds(pl.multiple_of(tile * 256, 256), 256)
        return pltpu.make_async_copy(spec.at[:, cols], spec_hbm.at[:, cols], out_sem.at[tile])

    @pl.loop(0, NY // 256)
    def _(tile):
        cols = pl.ds(pl.multiple_of(tile * 256, 256), 256)
        spec[:, cols] = jnp.dot(left[...], second[:, cols], preferred_element_type=F32)
        write(tile).start()

    @pl.loop(0, NY // 256)
    def _(tile):
        write(tile).wait()


def update_kernel(shift_ref, spec_ref, q_ref, u_ref, at_ref, count_ref, tvel_ref, q_out, u_out, t_out):
    rows = q_ref.shape[2]
    kz_first = lax.axis_index("gy") * KZL + pl.program_id(0) * rows
    shift = shift_ref[0]
    ky = lane_index((rows, NY))
    kys = jnp.where(ky < NY // 2, ky, ky - NY).astype(F32)
    kz = (lax.broadcasted_iota(jnp.int32, (rows, NY), 0) + kz_first).astype(F32)
    wave_square = kz * kz + kys * kys
    inverse = 1.0 / jnp.maximum(wave_square, 1.0)
    scale = 1.0 / math.sqrt(NY * NZ)
    damping = (time_step * scale) * jnp.exp(-2.0 * wave_square / (NY * NZ))
    for part in range(2):
        moved = [pltpu.roll(spec_ref[part, comp], shift, 1) for comp in range(3)]
        radial = (kys * moved[1] + kz * moved[2]) * inverse
        projected = [moved[0], moved[1] - kys * radial, moved[2] - kz * radial]
        for comp in range(3):
            q_new = coef_keep * q_ref[part, comp] + damping * projected[comp]
            q_out[part, comp] = q_new
            u_out[part, comp] = u_ref[part, comp] + coef_add * q_new

    counts = jnp.broadcast_to(count_ref[...], (DEV, DEV))
    diagonal = lax.broadcasted_iota(jnp.int32, (DEV, DEV), 0) == lax.broadcasted_iota(jnp.int32, (DEV, DEV), 1)
    count_col = jnp.sum(jnp.where(diagonal, counts, 0).astype(F32), axis=1, keepdims=True)
    alive = (lane_index((DEV, TPP)).astype(F32) < count_col).astype(F32)
    for comp in range(3):
        old = tvel_ref[comp]
        at = jnp.concatenate([at_ref[peer, comp : comp + 1, 0:TPP] for peer in range(DEV)], axis=0)
        t_out[comp] = old + relax_ratio * alive * (at - old)


def on_device(
    velocity,
    vorticity,
    q_state,
    u_state,
    shift,
    requests,
    tracer_slot,
    tracer_row,
    tracer_col,
    tracer_count,
    tracer_frac,
    tracer_vel,
):
    first, second = tables()
    hbm = pl.BlockSpec(memory_space=pl.ANY)
    vmem = pl.BlockSpec(memory_space=pltpu.VMEM)
    count = tracer_count.reshape(1, DEV)
    old = tracer_vel.reshape(3, DEV, TPP)
    spectrum, at_tracer = pl.pallas_call(
        exchange_kernel,
        out_shape=(
            jax.ShapeDtypeStruct((6 * KZL, NY), F32),
            jax.ShapeDtypeStruct((DEV, 8, 128), F32),
        ),
        in_specs=[hbm] * 4 + [vmem] * 7,
        out_specs=(hbm, vmem),
        scratch_shapes=[
            pltpu.VMEM((3, PLANES, LOC, LOC), F32),
            pltpu.VMEM((3, PLANES, LOC, LOC), F32),
            pltpu.VMEM((DEV * 128, DEV * 128), BF16),
            pltpu.VMEM((2 * NY, NY), BF16),
            pltpu.VMEM((PLANES * LOC, 384), BF16),
            pltpu.VMEM((2 * TR, PLANES * LOC), BF16),
            pltpu.VMEM((2 * TR, 384), F32),
            pltpu.VMEM((2 * TR, 768), BF16),
            pltpu.VMEM((TR, 128), F32),
            pltpu.VMEM((8, TR), F32),
            pltpu.VMEM((TR, 128), F32),
            pltpu.VMEM((DEV, 8, 128), F32),
            pltpu.VMEM((DEV, 8, 128), F32),
            pltpu.VMEM((DEV, 8, 128), F32),
            pltpu.VMEM((DEV, 8, 128), F32),
            pltpu.VMEM((DEV, PIECE, 128), BF16),
            pltpu.VMEM((WIDE, DEV * 128), BF16),
            pltpu.VMEM((DEV, PIECE, 128), BF16),
            pltpu.VMEM((DEV, PIECE, 128), BF16),
            pltpu.VMEM((6 * KZL, 2 * NY), BF16),
            pltpu.VMEM((6 * KZL, NY), F32),
            pltpu.SemaphoreType.DMA((4,)),
            pltpu.SemaphoreType.DMA((4,)),
            pltpu.SemaphoreType.DMA((NY // 256,)),
        ]
        + [pltpu.SemaphoreType.DMA((DEV,))] * 8,
        compiler_params=pltpu.CompilerParams(
            collective_id=0, has_side_effects=True, vmem_limit_bytes=56 * 2**20
        ),
        cost_estimate=pl.CostEstimate(flops=6 * 10**9, bytes_accessed=25 * 2**20, transcendentals=0),
        name="exchange",
    )(
        velocity,
        vorticity,
        jnp.asarray(first),
        jnp.asarray(second),
        requests.reshape(DEV, 4),
        tracer_slot.reshape(DEV, TPP),
        tracer_row.reshape(DEV, TPP),
        tracer_col.reshape(DEV, TPP),
        count,
        tracer_frac.reshape(2, DEV, TPP),
        old,
    )
    rows = 8
    part = pl.BlockSpec((2, 3, rows, NY), lambda i: (0, 0, i, 0))

    def whole(*shape):
        return pl.BlockSpec(shape, lambda i: (0,) * len(shape))

    q_next, u_next, tracer_next = pl.pallas_call(
        update_kernel,
        grid=(KZL // rows,),
        out_shape=(
            jax.ShapeDtypeStruct((2, 3, KZL, NY), F32),
            jax.ShapeDtypeStruct((2, 3, KZL, NY), F32),
            jax.ShapeDtypeStruct((3, DEV, TPP), F32),
        ),
        in_specs=[
            pl.BlockSpec(memory_space=pltpu.SMEM),
            part,
            part,
            part,
            whole(DEV, 8, 128),
            whole(1, DEV),
            whole(3, DEV, TPP),
        ],
        out_specs=(part, part, whole(3, DEV, TPP)),
        compiler_params=pltpu.CompilerParams(vmem_limit_bytes=32 * 2**20),
        name="update",
    )(
        shift,
        spectrum.reshape(2, 3, KZL, NY),
        q_state.reshape(2, 3, KZL, NY),
        u_state.reshape(2, 3, KZL, NY),
        at_tracer,
        count,
        old,
    )
    return (
        q_next.reshape(q_state.shape),
        u_next.reshape(u_state.shape),
        tracer_next.reshape(tracer_vel.shape),
    )


def solution(mesh):
    return jax.shard_map(
        on_device,
        mesh=mesh,
        in_specs=(
            P(None, None, "gy", "gz"),
            P(None, None, "gy", "gz"),
            P(None, None, "gz", "gy", None),
            P(None, None, "gz", "gy", None),
            P("gz"),
            P("gy", "gz", None, None),
            P("gy", "gz", None, None),
            P("gy", "gz", None, None),
            P("gy", "gz", None, None),
            P("gy", "gz", None),
            P(None, "gy", "gz", None, None),
            P(None, "gy", "gz", None, None),
        ),
        out_specs=(
            P(None, None, "gz", "gy", None),
            P(None, None, "gz", "gy", None),
            P(None, "gy", "gz", None, None),
        ),
        check_vma=False,
    )
```

```python
import functools
import math

import jax
import jax.numpy as jnp
import ml_dtypes
import numpy as np
from jax import lax
from jax.experimental import pallas as pl
from jax.experimental.pallas import tpu as pltpu
from jax.sharding import PartitionSpec as P

MESH = pl.DeviceIdType.MESH
BF16 = jnp.bfloat16
F32 = jnp.float32

NY = 1536
NZ = 1536
DEV = 16
LOC = 96
PLANES = 16
CELL_ROWS = PLANES * LOC
BLOCKS = 192
KZL = 48
TPP = 32
TR = DEV * TPP
QUARTER = 24
SPLIT = ((0, 16), (16, 8))
MAIN = (144, 72)
PIECE = (144, 80)
LAST = (48, 24)
WIDE = (192, 112)
DEPTH = (2048, 1024)

drag_mass = 24.0
relax_ratio = 0.5
coef_keep = -5.0 / 9.0
coef_add = 15.0 / 16.0
time_step = 0.5


def dft_base(length):
    index = np.arange(length, dtype=np.int64)
    phase = (np.outer(index, index) % length).astype(np.float32) * np.float32(2.0 * math.pi / length)
    return np.cos(phase).astype(ml_dtypes.bfloat16), np.sin(phase).astype(ml_dtypes.bfloat16)


@functools.lru_cache(maxsize=None)
def tables():
    cos, sin = dft_base(NY)
    first = np.zeros((DEV, 128, DEV, 128), ml_dtypes.bfloat16)
    kz_cos = cos[:, : NZ // 2].reshape(DEV, LOC, DEV, KZL)
    kz_sin = sin[:, : NZ // 2].reshape(DEV, LOC, DEV, KZL)
    first[:, :LOC, :, :KZL] = kz_cos
    first[:, :LOC, :, KZL : 2 * KZL] = -kz_sin
    second = []
    for low, rows in SPLIT:
        quarter = np.arange(4)[:, None, None]
        source = np.arange(DEV)[None, :, None]
        row = np.arange(rows)[None, None, :]
        row_of = (source * LOC + quarter * QUARTER + low + row).reshape(-1)
        second += [cos[row_of], sin[row_of]]
    return first.reshape(DEV * 128, DEV * 128), np.concatenate(second, axis=0)


def lane_index(shape):
    return lax.broadcasted_iota(jnp.int32, shape, len(shape) - 1)


def pack(main, last, part):
    rows = SPLIT[part][1]
    lane = lane_index((rows, 128))
    out = []
    for comp in range(3):
        low = last[comp * rows : (comp + 1) * rows]
        for third in range(3):
            at = (comp * 3 + third) * rows
            turned = pltpu.roll(low, 96 - 32 * third, 1)
            out.append(jnp.where(lane < LOC, main[at : at + rows], turned))
    if PIECE[part] > MAIN[part]:
        out.append(jnp.zeros((PIECE[part] - MAIN[part], 128), F32))
    return jnp.concatenate(out, axis=0)


def unpack_last(piece, part):
    rows = SPLIT[part][1]
    lane = lane_index((rows, 128))
    out = []
    for comp in range(3):
        parts = [
            pltpu.roll(
                piece[(comp * 3 + third) * rows : (comp * 3 + third + 1) * rows], (32 * third + 32) % 128, 1
            )
            for third in range(3)
        ]
        out.append(
            jnp.where(lane < 32, parts[0], jnp.where(lane < 64, parts[1], jnp.where(lane < LOC, parts[2], 0.0)))
        )
    rest = WIDE[part] - PIECE[part] - LAST[part]
    if rest:
        out.append(jnp.zeros((rest, 128), F32))
    return jnp.concatenate(out, axis=0)


def widen(block):
    return jnp.concatenate([block, jnp.zeros((block.shape[0], 128 - block.shape[1]), block.dtype)], axis=1)


def exchange_kernel(
    vel_hbm,
    vort_hbm,
    first_hbm,
    second_hbm,
    requests_ref,
    slot_ref,
    row_ref,
    col_ref,
    count_ref,
    frac_ref,
    tvel_ref,
    spec_hbm,
    at_ref,
    vel,
    vort,
    cross,
    first,
    second,
    vel_b,
    hot,
    picked,
    spread,
    row_lanes,
    t_send,
    t_recv,
    a_send,
    a_recv,
    send1a,
    send1b,
    recv1a,
    recv1b,
    send2a,
    send2b,
    recv2a,
    recv2b,
    left_a,
    left_b,
    spec,
    load_sem,
    own_sem,
    out_sem,
    t_ssem,
    t_rsem,
    a_ssem,
    a_rsem,
    ssem1a,
    rsem1a,
    ssem1b,
    rsem1b,
    ssem2a,
    rsem2a,
    ssem2b,
    rsem2b,
):
    gy = lax.axis_index("gy")
    gz = lax.axis_index("gz")
    my_x, my_h = gz // 4, lax.rem(gz, 4)
    send1, recv1 = (send1a, send1b), (recv1a, recv1b)
    send2, recv2 = (send2a, send2b), (recv2a, recv2b)
    sems1 = ((ssem1a, rsem1a), (ssem1b, rsem1b))
    sems2 = ((ssem2a, rsem2a), (ssem2b, rsem2b))
    left = (left_a, left_b)

    def along(base, step):
        return lax.rem(base + step, DEV)

    barrier = pltpu.get_barrier_semaphore()
    for step in range(1, DEV):
        pl.semaphore_signal(barrier, inc=1, device_id=(gy, along(gz, step)), device_id_type=MESH)
    for step in range(1, DEV):
        pl.semaphore_signal(barrier, inc=1, device_id=(along(gy, step), gz), device_id_type=MESH)
    loads = [
        pltpu.make_async_copy(vel_hbm, vel, load_sem.at[0]),
        pltpu.make_async_copy(vort_hbm, vort, load_sem.at[1]),
        pltpu.make_async_copy(first_hbm, first, load_sem.at[2]),
        pltpu.make_async_copy(second_hbm, second, load_sem.at[3]),
    ]
    for load in loads:
        load.start()

    slots = slot_ref[...]
    wanted = requests_ref[...]
    block = jnp.zeros((DEV, TPP), jnp.int32)
    for number in range(4):
        block = jnp.where(slots == number, wanted[:, number : number + 1], block)
    counts = jnp.broadcast_to(count_ref[...], (DEV, DEV))
    diagonal = lax.broadcasted_iota(jnp.int32, (DEV, DEV), 0) == lax.broadcasted_iota(jnp.int32, (DEV, DEV), 1)
    count_col = jnp.sum(jnp.where(diagonal, counts, 0).astype(F32), axis=1, keepdims=True)
    alive = (lane_index((DEV, TPP)).astype(F32) < count_col).astype(F32)
    upper = [(block * 8 + row_ref[...]).astype(F32), col_ref[...].astype(F32), frac_ref[0], frac_ref[1]]
    lower = [tvel_ref[0], tvel_ref[1], tvel_ref[2], alive]
    t_send[:, 0, :] = jnp.concatenate(upper, axis=1)
    t_send[:, 1, :] = jnp.concatenate(lower, axis=1)

    pl.semaphore_wait(barrier, 2 * (DEV - 1))

    def to_holder(step):
        peer = along(gz, step)
        return pltpu.make_async_remote_copy(
            src_ref=t_send.at[peer],
            dst_ref=t_recv.at[gz],
            send_sem=t_ssem.at[step],
            recv_sem=t_rsem.at[step],
            device_id=(gy, peer),
            device_id_type=MESH,
        )

    for step in range(1, DEV):
        to_holder(step).start()
    own = pltpu.make_async_copy(t_send.at[gz], t_recv.at[gz], own_sem.at[0])
    own.start()

    loads[0].wait()
    for comp in range(3):
        for row in range(8):
            cols = slice(comp * 1024 + row * 128, comp * 1024 + (row + 1) * 128)
            vel_b[0:BLOCKS, cols] = widen(vel[comp, pl.ds(row, BLOCKS, stride=8), :]).astype(BF16)
    vel_b[BLOCKS:256, :] = jnp.zeros((256 - BLOCKS, 3072), BF16)
    loads[1].wait()

    @pl.loop(0, PLANES)
    def _(plane):
        rows = pl.ds(pl.multiple_of(plane * LOC, LOC), LOC)
        u = [vel[comp, rows, :] for comp in range(3)]
        w = [vort[comp, rows, :] for comp in range(3)]
        for comp in range(3):
            a, b = (comp + 1) % 3, (comp + 2) % 3
            cross[plane, comp * LOC : (comp + 1) * LOC, :] = widen(u[a] * w[b] - u[b] * w[a])

    own.wait()
    for step in range(1, DEV):
        to_holder(step).wait()

    upper = t_recv[:, 0, :]
    lower = t_recv[:, 1, :]
    turned = jnp.concatenate([upper, lower, jnp.zeros((128 - 2 * DEV, 128), F32)], axis=0).T
    lane_row = lane_index((1, 128))
    for quad in range(4):
        total = jnp.zeros((1, 128), F32)
        for number in range(4):
            owner = quad * 4 + number
            total = jnp.where(
                lane_row // TPP == number, pltpu.roll(upper[owner : owner + 1], number * TPP, 1), total
            )
        row_lanes[0:1, quad * 128 : (quad + 1) * 128] = total

    def field(number, owner):
        rows = slice((number % 4) * TPP, (number % 4 + 1) * TPP)
        col = (number // 4) * DEV + owner
        return jnp.broadcast_to(turned[rows, col : col + 1], (TPP, 128))

    lane = lane_index((TPP, 128))
    lane_f = lane.astype(F32)
    for owner in range(DEV):
        block_at = (field(0, owner).astype(jnp.int32) // 8)
        rows = slice(owner * TPP, (owner + 1) * TPP)
        hot[rows, 0:128] = jnp.where(lane == block_at, 1.0, 0.0).astype(BF16)
        hot[rows, 128:256] = jnp.where(lane + 128 == block_at, 1.0, 0.0).astype(BF16)

    @pl.loop(0, 6)
    def _(tile):
        cols = pl.ds(pl.multiple_of(tile * 512, 512), 512)
        picked[:, cols] = jnp.dot(hot[...], vel_b[:, cols], preferred_element_type=F32)

    back = jnp.zeros((TPP, 128), F32)
    for owner in range(DEV):
        rows = slice(owner * TPP, (owner + 1) * TPP)
        lows = slice(TR + owner * TPP, TR + (owner + 1) * TPP)
        row = jnp.bitwise_and(field(0, owner).astype(jnp.int32), 7)
        start, along_y, along_z = field(1, owner), field(2, owner), field(3, owner)
        cell = jnp.where(lane_f == start, 1.0 - along_z, jnp.where(lane_f == start + 1.0, along_z, 0.0))
        upper_w = (1.0 - along_y) * cell
        lower_w = along_y * cell
        picks = [
            jnp.where(row == number, 1.0 - along_y, jnp.where(row + 1 == number, along_y, 0.0))
            for number in range(8)
        ]
        mass = drag_mass * field(7, owner)
        for comp in range(3):
            line = picks[0] * picked[rows, comp * 1024 : comp * 1024 + 128]
            for number in range(1, 8):
                line += picks[number] * picked[rows, comp * 1024 + number * 128 : comp * 1024 + (number + 1) * 128]
            at = jnp.sum(cell * line, axis=1, keepdims=True)
            back = jnp.where(lane == comp * DEV + owner, at, back)
            drag = mass * (field(4 + comp, owner) - at)
            for weight, place in ((upper_w, rows), (lower_w, lows)):
                value = weight * drag
                high = value.astype(BF16)
                spread[place, comp * 256 : comp * 256 + 128] = high
                spread[place, comp * 256 + 128 : (comp + 1) * 256] = (value - high.astype(F32)).astype(BF16)

    def far(number):
        return jnp.where(number == 0, 2, jnp.where(number == 1, 1, jnp.where(number == 2, 3, 0)))

    def plane_of(step):
        dx, dh = far(lax.rem(step, 4)), far(step // 4)
        return lax.rem(my_x + dx, 4) * 4 + lax.rem(my_h + dh, 4)

    def landing(part):
        return recv1[part].at[pl.ds(0, PIECE[part]), pl.ds(pl.multiple_of(gz * 128, 128), 128)]

    def to_plane(step, part):
        peer = plane_of(step)
        return pltpu.make_async_remote_copy(
            src_ref=send1[part].at[peer],
            dst_ref=landing(part),
            send_sem=sems1[part][0].at[step],
            recv_sem=sems1[part][1].at[step],
            device_id=(gy, peer),
            device_id_type=MESH,
        )

    def own_plane(part):
        return pltpu.make_async_copy(send1[part].at[gz], landing(part), own_sem.at[1 + part])

    starts = row_lanes[0:1, :]

    @pl.loop(0, DEV // 2)
    def _(turn):
        planes = [plane_of(2 * turn), plane_of(2 * turn + 1)]
        hots = []
        for plane in planes:
            cell_row = (lax.broadcasted_iota(jnp.int32, (LOC, TR), 0) + plane * LOC).astype(F32)
            up = jnp.where(cell_row == starts, 1.0, 0.0).astype(BF16)
            down = jnp.where(cell_row == starts + 1.0, 1.0, 0.0).astype(BF16)
            hots.append(jnp.concatenate([up, down], axis=1))
        both = jnp.concatenate(hots, axis=0)
        forces = [[], []]
        for comp in range(3):
            fed = jnp.dot(both, spread[:, comp * 256 : (comp + 1) * 256], preferred_element_type=F32)
            for half in range(2):
                mine = fed[half * LOC : (half + 1) * LOC]
                forces[half].append(
                    cross[planes[half], comp * LOC : (comp + 1) * LOC, :] + (mine[:, 0:128] + mine[:, 128:256])
                )
        for half in range(2):
            for part in range(2):
                low, rows = SPLIT[part]
                main = [
                    forces[half][comp][third * QUARTER + low : third * QUARTER + low + rows]
                    for comp in range(3)
                    for third in range(3)
                ]
                last = [forces[half][comp][72 + low : 72 + low + rows] for comp in range(3)]
                send1[part][planes[half]] = pack(
                    jnp.concatenate(main, axis=0), jnp.concatenate(last, axis=0), part
                ).astype(BF16)
        to_plane(2 * turn, 0).start()

        @pl.when(turn < DEV // 2 - 1)
        def _():
            to_plane(2 * turn + 1, 0).start()

    own_plane(0).start()

    @pl.loop(0, DEV - 1)
    def _(step):
        to_plane(step, 1).start()

    own_plane(1).start()

    done = jnp.concatenate([back, jnp.zeros((128 - TPP, 128), F32)], axis=0).T
    a_send[:, 0, :] = (
        done[0:DEV] + pltpu.roll(done[DEV : 2 * DEV], TPP, 1) + pltpu.roll(done[2 * DEV : 3 * DEV], 2 * TPP, 1)
    )

    def to_owner(step):
        peer = along(gz, step)
        return pltpu.make_async_remote_copy(
            src_ref=a_send.at[peer],
            dst_ref=a_recv.at[gz],
            send_sem=a_ssem.at[step],
            recv_sem=a_rsem.at[step],
            device_id=(gy, peer),
            device_id_type=MESH,
        )

    for step in range(1, DEV):
        to_owner(step).start()
    own_at = pltpu.make_async_copy(a_send.at[gz], a_recv.at[gz], own_sem.at[3])
    own_at.start()

    def to_waves(step, part):
        peer = lax.rem(gy // 2 + step // 2, 8) * 2 + lax.rem(gy + step, 2)
        return pltpu.make_async_remote_copy(
            src_ref=send2[part].at[peer],
            dst_ref=recv2[part].at[gy],
            send_sem=sems2[part][0].at[step],
            recv_sem=sems2[part][1].at[step],
            device_id=(peer, gz),
            device_id_type=MESH,
        )

    def own_waves(part):
        return pltpu.make_async_copy(send2[part].at[gy], recv2[part].at[gy], own_sem.at[4 + part])

    def make_pair(turn, part):
        pair = lax.rem(gy // 2 + turn, 8)
        cols = pl.ds(pl.multiple_of(pair * 256, 256), 256)
        out = jnp.dot(recv1[part][...], first[:, cols], preferred_element_type=F32)
        for half in range(2):
            lanes = slice(half * 128, (half + 1) * 128)
            main = out[0 : MAIN[part], lanes]
            last = out[PIECE[part] : PIECE[part] + LAST[part], lanes]
            send2[part][pair * 2 + half] = pack(main, last, part).astype(BF16)

    def z_transform(part):
        own_plane(part).wait()

        @pl.loop(0, DEV - 1)
        def _(step):
            to_plane(step, part).wait()

        @pl.loop(0, DEV)
        def _(source):
            cols = pl.ds(pl.multiple_of(source * 128, 128), 128)
            piece = recv1[part][0 : PIECE[part], cols].astype(F32)
            recv1[part][PIECE[part] : WIDE[part], cols] = unpack_last(piece, part).astype(BF16)

        @pl.loop(1, 8)
        def _(turn):
            make_pair(turn, part)
            to_waves(2 * turn, part).start()
            to_waves(2 * turn + 1, part).start()

        make_pair(0, part)
        to_waves(1, part).start()
        own_waves(part).start()

    loads[2].wait()
    z_transform(0)
    z_transform(1)

    def y_lines(part):
        own_waves(part).wait()

        @pl.loop(1, DEV)
        def _(step):
            to_waves(step, part).wait()

        rows = SPLIT[part][1]
        depth = DEPTH[part] // 2
        quarter = depth // 4
        for comp in range(3):
            re_at, im_at = comp * KZL, (3 + comp) * KZL
            for third in range(3):
                at = (comp * 3 + third) * rows
                stacked = recv2[part][...].astype(F32)[:, at : at + rows].reshape(DEV * rows, 128)
                for piece in range(DEV * rows // 128):
                    tile = stacked[piece * 128 : (piece + 1) * 128].T
                    lo = third * quarter + piece * 128
                    cols, more = slice(lo, lo + 128), slice(depth + lo, depth + lo + 128)
                    real, imag = tile[0:KZL].astype(BF16), tile[KZL : 2 * KZL].astype(BF16)
                    left[part][re_at : re_at + KZL, cols] = real
                    left[part][re_at : re_at + KZL, more] = imag
                    left[part][im_at : im_at + KZL, cols] = imag
                    left[part][im_at : im_at + KZL, more] = -real
                    lo = 3 * quarter + piece * 128
                    cols, more = slice(lo, lo + 128), slice(depth + lo, depth + lo + 128)
                    for half in range(2):
                        value = tile[96 + half * 16 : 112 + half * 16].astype(BF16)
                        kz = third * 32 + half * 16
                        if kz < KZL:
                            left[part][re_at + kz : re_at + kz + 16, cols] = value
                            left[part][im_at + kz : im_at + kz + 16, more] = -value
                        else:
                            kz -= KZL
                            left[part][re_at + kz : re_at + kz + 16, more] = value
                            left[part][im_at + kz : im_at + kz + 16, cols] = value

    loads[3].wait()
    y_lines(0)

    @pl.loop(0, NY // 256)
    def _(tile):
        cols = pl.ds(pl.multiple_of(tile * 256, 256), 256)
        spec[:, cols] = jnp.dot(left_a[...], second[0 : DEPTH[0], cols], preferred_element_type=F32)

    own_at.wait()
    for step in range(1, DEV):
        to_owner(step).wait()
    at_ref[...] = a_recv[:, 0, :]

    y_lines(1)

    def write(tile):
        cols = pl.ds(pl.multiple_of(tile * 256, 256), 256)
        return pltpu.make_async_copy(spec.at[:, cols], spec_hbm.at[:, cols], out_sem.at[tile])

    @pl.loop(0, NY // 256)
    def _(tile):
        cols = pl.ds(pl.multiple_of(tile * 256, 256), 256)
        spec[:, cols] += jnp.dot(left_b[...], second[DEPTH[0] :, cols], preferred_element_type=F32)
        write(tile).start()

    @pl.loop(0, NY // 256)
    def _(tile):
        write(tile).wait()


def update_kernel(shift_ref, spec_ref, q_ref, u_ref, at_ref, count_ref, tvel_ref, q_out, u_out, t_out):
    rows = q_ref.shape[2]
    kz_first = lax.axis_index("gy") * KZL + pl.program_id(0) * rows
    shift = shift_ref[0]
    tiles_on, lanes_on = shift // 128, lax.rem(shift, 128)
    scale = 1.0 / math.sqrt(NY * NZ)
    kz = (lax.broadcasted_iota(jnp.int32, (rows, 128), 0) + kz_first).astype(F32)
    lane = lane_index((rows, 128))
    early = lane < lanes_on

    def turned(part, comp, tile):
        at = lax.rem(tile + 24 - tiles_on, 12)
        before = lax.rem(at + 11, 12)
        pieces = [
            spec_ref[part, comp, :, pl.ds(pl.multiple_of(place * 128, 128), 128)] for place in (before, at)
        ]
        return pltpu.roll(jnp.where(lane >= 128 - lanes_on, pieces[0], pieces[1]), lanes_on, 1)

    for tile in range(NY // 128):
        cols = slice(tile * 128, (tile + 1) * 128)
        kys = (lane + (tile * 128 if tile < 6 else tile * 128 - NY)).astype(F32)
        wave_square = kz * kz + kys * kys
        inverse = 1.0 / jnp.maximum(wave_square, 1.0)
        damping = (time_step * scale) * jnp.exp(-2.0 * wave_square / (NY * NZ))
        for part in range(2):
            moved = [turned(part, comp, tile) for comp in range(3)]
            radial = (kys * moved[1] + kz * moved[2]) * inverse
            projected = [moved[0], moved[1] - kys * radial, moved[2] - kz * radial]
            for comp in range(3):
                q_new = coef_keep * q_ref[part, comp, :, cols] + damping * projected[comp]
                q_out[part, comp, :, cols] = q_new
                u_out[part, comp, :, cols] = u_ref[part, comp, :, cols] + coef_add * q_new

    @pl.when(pl.program_id(0) == 0)
    def _():
        counts = jnp.broadcast_to(count_ref[...], (DEV, DEV))
        diagonal = lax.broadcasted_iota(jnp.int32, (DEV, DEV), 0) == lax.broadcasted_iota(jnp.int32, (DEV, DEV), 1)
        count_col = jnp.sum(jnp.where(diagonal, counts, 0).astype(F32), axis=1, keepdims=True)
        alive = (lane_index((DEV, TPP)).astype(F32) < count_col).astype(F32)
        for comp in range(3):
            old = tvel_ref[comp]
            at = at_ref[:, comp * TPP : (comp + 1) * TPP]
            t_out[comp] = old + relax_ratio * alive * (at - old)


def on_device(
    velocity,
    vorticity,
    q_state,
    u_state,
    shift,
    requests,
    tracer_slot,
    tracer_row,
    tracer_col,
    tracer_count,
    tracer_frac,
    tracer_vel,
):
    first, second = tables()
    hbm = pl.BlockSpec(memory_space=pl.ANY)
    vmem = pl.BlockSpec(memory_space=pltpu.VMEM)
    count = tracer_count.reshape(1, DEV)
    old = tracer_vel.reshape(3, DEV, TPP)
    spectrum, at_tracer = pl.pallas_call(
        exchange_kernel,
        out_shape=(
            jax.ShapeDtypeStruct((6 * KZL, NY), F32),
            jax.ShapeDtypeStruct((DEV, 128), F32),
        ),
        in_specs=[hbm] * 4 + [vmem] * 7,
        out_specs=(hbm, vmem),
        scratch_shapes=[
            pltpu.VMEM((3, CELL_ROWS, LOC), F32),
            pltpu.VMEM((3, CELL_ROWS, LOC), F32),
            pltpu.VMEM((PLANES, 3 * LOC, 128), F32),
            pltpu.VMEM((DEV * 128, DEV * 128), BF16),
            pltpu.VMEM((2 * NY, NY), BF16),
            pltpu.VMEM((256, 3072), BF16),
            pltpu.VMEM((TR, 256), BF16),
            pltpu.VMEM((TR, 3072), F32),
            pltpu.VMEM((2 * TR, 768), BF16),
            pltpu.VMEM((8, TR), F32),
            pltpu.VMEM((DEV, 2, 128), F32),
            pltpu.VMEM((DEV, 2, 128), F32),
            pltpu.VMEM((DEV, 1, 128), F32),
            pltpu.VMEM((DEV, 1, 128), F32),
            pltpu.VMEM((DEV, PIECE[0], 128), BF16),
            pltpu.VMEM((DEV, PIECE[1], 128), BF16),
            pltpu.VMEM((WIDE[0], DEV * 128), BF16),
            pltpu.VMEM((WIDE[1], DEV * 128), BF16),
            pltpu.VMEM((DEV, PIECE[0], 128), BF16),
            pltpu.VMEM((DEV, PIECE[1], 128), BF16),
            pltpu.VMEM((DEV, PIECE[0], 128), BF16),
            pltpu.VMEM((DEV, PIECE[1], 128), BF16),
            pltpu.VMEM((6 * KZL, DEPTH[0]), BF16),
            pltpu.VMEM((6 * KZL, DEPTH[1]), BF16),
            pltpu.VMEM((6 * KZL, NY), F32),
            pltpu.SemaphoreType.DMA((4,)),
            pltpu.SemaphoreType.DMA((6,)),
            pltpu.SemaphoreType.DMA((NY // 256,)),
        ]
        + [pltpu.SemaphoreType.DMA((DEV,))] * 12,
        compiler_params=pltpu.CompilerParams(
            collective_id=0, has_side_effects=True, vmem_limit_bytes=56 * 2**20
        ),
        cost_estimate=pl.CostEstimate(flops=6 * 10**9, bytes_accessed=25 * 2**20, transcendentals=0),
        name="exchange",
    )(
        velocity.reshape(3, CELL_ROWS, LOC),
        vorticity.reshape(3, CELL_ROWS, LOC),
        jnp.asarray(first),
        jnp.asarray(second),
        requests.reshape(DEV, 4),
        tracer_slot.reshape(DEV, TPP),
        tracer_row.reshape(DEV, TPP),
        tracer_col.reshape(DEV, TPP),
        count,
        tracer_frac.reshape(2, DEV, TPP),
        old,
    )
    rows = 8
    part = pl.BlockSpec((2, 3, rows, NY), lambda i: (0, 0, i, 0))

    def whole(*shape):
        return pl.BlockSpec(shape, lambda i: (0,) * len(shape))

    q_next, u_next, tracer_next = pl.pallas_call(
        update_kernel,
        grid=(KZL // rows,),
        out_shape=(
            jax.ShapeDtypeStruct((2, 3, KZL, NY), F32),
            jax.ShapeDtypeStruct((2, 3, KZL, NY), F32),
            jax.ShapeDtypeStruct((3, DEV, TPP), F32),
        ),
        in_specs=[
            pl.BlockSpec(memory_space=pltpu.SMEM),
            part,
            part,
            part,
            whole(DEV, 128),
            whole(1, DEV),
            whole(3, DEV, TPP),
        ],
        out_specs=(part, part, whole(3, DEV, TPP)),
        compiler_params=pltpu.CompilerParams(vmem_limit_bytes=60 * 2**20),
        name="update",
    )(
        shift,
        spectrum.reshape(2, 3, KZL, NY),
        q_state.reshape(2, 3, KZL, NY),
        u_state.reshape(2, 3, KZL, NY),
        at_tracer,
        count,
        old,
    )
    return (
        q_next.reshape(q_state.shape),
        u_next.reshape(u_state.shape),
        tracer_next.reshape(tracer_vel.shape),
    )


def solution(mesh):
    return jax.shard_map(
        on_device,
        mesh=mesh,
        in_specs=(
            P(None, None, "gy", "gz"),
            P(None, None, "gy", "gz"),
            P(None, None, "gz", "gy", None),
            P(None, None, "gz", "gy", None),
            P("gz"),
            P("gy", "gz", None, None),
            P("gy", "gz", None, None),
            P("gy", "gz", None, None),
            P("gy", "gz", None, None),
            P("gy", "gz", None),
            P(None, "gy", "gz", None, None),
            P(None, "gy", "gz", None, None),
        ),
        out_specs=(
            P(None, None, "gz", "gy", None),
            P(None, None, "gz", "gy", None),
            P(None, "gy", "gz", None, None),
        ),
        check_vma=False,
    )
```

```python
import functools
import math

import jax
import jax.numpy as jnp
import ml_dtypes
import numpy as np
from jax import lax
from jax.experimental import pallas as pl
from jax.experimental.pallas import tpu as pltpu
from jax.sharding import PartitionSpec as P

MESH = pl.DeviceIdType.MESH
BF16 = jnp.bfloat16
F32 = jnp.float32

NY = 1536
NZ = 1536
DEV = 16
LOC = 96
PLANES = 16
CELL_ROWS = PLANES * LOC
BLOCKS = 192
KZL = 48
TPP = 32
TR = DEV * TPP
QUARTER = 24
SPLIT = ((0, 16), (16, 8))
MAIN = (144, 72)
PIECE = (144, 80)
LAST = (48, 24)
WIDE = (192, 112)
ROWS = 8
DEPTH = (2048, 1024)

drag_mass = 24.0
relax_ratio = 0.5
coef_keep = -5.0 / 9.0
coef_add = 15.0 / 16.0
time_step = 0.5


def dft_base(length):
    index = np.arange(length, dtype=np.int64)
    phase = (np.outer(index, index) % length).astype(np.float32) * np.float32(2.0 * math.pi / length)
    return np.cos(phase).astype(ml_dtypes.bfloat16), np.sin(phase).astype(ml_dtypes.bfloat16)


@functools.lru_cache(maxsize=None)
def tables():
    cos, sin = dft_base(NY)
    first = np.zeros((DEV, 128, DEV, 128), ml_dtypes.bfloat16)
    kz_cos = cos[:, : NZ // 2].reshape(DEV, LOC, DEV, KZL)
    kz_sin = sin[:, : NZ // 2].reshape(DEV, LOC, DEV, KZL)
    first[:, :LOC, :, :KZL] = kz_cos
    first[:, :LOC, :, KZL : 2 * KZL] = -kz_sin
    second = []
    for low, rows in SPLIT:
        quarter = np.arange(4)[:, None, None]
        source = np.arange(DEV)[None, :, None]
        row = np.arange(rows)[None, None, :]
        row_of = (source * LOC + quarter * QUARTER + low + row).reshape(-1)
        second += [cos[row_of], sin[row_of]]
    return first.reshape(DEV * 128, DEV * 128), np.concatenate(second, axis=0)


def choose(number, values):
    out = values[-1]
    for place in range(len(values) - 2, -1, -1):
        out = jnp.where(number == place, values[place], out)
    return out


def lane_index(shape):
    return lax.broadcasted_iota(jnp.int32, shape, len(shape) - 1)


def pack(main, last, part):
    rows = SPLIT[part][1]
    lane = lane_index((rows, 128))
    out = []
    for comp in range(3):
        low = last[comp * rows : (comp + 1) * rows]
        for third in range(3):
            at = (comp * 3 + third) * rows
            turned = pltpu.roll(low, 96 - 32 * third, 1)
            out.append(jnp.where(lane < LOC, main[at : at + rows], turned))
    if PIECE[part] > MAIN[part]:
        out.append(jnp.zeros((PIECE[part] - MAIN[part], 128), F32))
    return jnp.concatenate(out, axis=0)


def unpack_last(piece, part):
    rows = SPLIT[part][1]
    lane = lane_index((rows, 128))
    out = []
    for comp in range(3):
        parts = [
            pltpu.roll(
                piece[(comp * 3 + third) * rows : (comp * 3 + third + 1) * rows], (32 * third + 32) % 128, 1
            )
            for third in range(3)
        ]
        out.append(
            jnp.where(lane < 32, parts[0], jnp.where(lane < 64, parts[1], jnp.where(lane < LOC, parts[2], 0.0)))
        )
    rest = WIDE[part] - PIECE[part] - LAST[part]
    if rest:
        out.append(jnp.zeros((rest, 128), F32))
    return jnp.concatenate(out, axis=0)


def widen(block):
    return jnp.concatenate([block, jnp.zeros((block.shape[0], 128 - block.shape[1]), block.dtype)], axis=1)


def as_column(row):
    spread = jnp.broadcast_to(row, (DEV, DEV)).astype(F32)
    diagonal = lax.broadcasted_iota(jnp.int32, (DEV, DEV), 0) == lax.broadcasted_iota(jnp.int32, (DEV, DEV), 1)
    return jnp.sum(jnp.where(diagonal, spread, 0.0), axis=1, keepdims=True)


def exchange_kernel(
    vel_hbm,
    vort_hbm,
    first_hbm,
    second_hbm,
    requests_hbm,
    slot_hbm,
    row_hbm,
    col_hbm,
    count_hbm,
    frac_hbm,
    tvel_hbm,
    spec_hbm,
    at_ref,
    requests_ref,
    slot_ref,
    row_ref,
    col_ref,
    count_ref,
    frac_ref,
    tvel_ref,
    vel,
    vort,
    cross,
    first,
    second,
    vel_b,
    hot,
    picked,
    spread,
    row_lanes,
    t_send,
    t_recv,
    a_send,
    a_recv,
    send1a,
    send1b,
    recv1a,
    recv1b,
    send2a,
    send2b,
    recv2a,
    recv2b,
    left_a,
    left_b,
    spec,
    load_sem,
    small_sem,
    own_sem,
    out_sem,
    t_ssem,
    t_rsem,
    a_ssem,
    a_rsem,
    ssem1a,
    rsem1a,
    ssem1b,
    rsem1b,
    ssem2a,
    rsem2a,
    ssem2b,
    rsem2b,
):
    gy = lax.axis_index("gy")
    gz = lax.axis_index("gz")
    my_x, my_h = gz // 4, lax.rem(gz, 4)
    send1, recv1 = (send1a, send1b), (recv1a, recv1b)
    send2, recv2 = (send2a, send2b), (recv2a, recv2b)
    sems1 = ((ssem1a, rsem1a), (ssem1b, rsem1b))
    sems2 = ((ssem2a, rsem2a), (ssem2b, rsem2b))
    left = (left_a, left_b)

    def along(base, step):
        return lax.rem(base + step, DEV)

    barrier = pltpu.get_barrier_semaphore()
    for step in range(1, DEV):
        pl.semaphore_signal(barrier, inc=1, device_id=(gy, along(gz, step)), device_id_type=MESH)
    for step in range(1, DEV):
        pl.semaphore_signal(barrier, inc=1, device_id=(along(gy, step), gz), device_id_type=MESH)
    loads = [
        pltpu.make_async_copy(vel_hbm, vel, load_sem.at[0]),
        pltpu.make_async_copy(vort_hbm, vort, load_sem.at[1]),
        pltpu.make_async_copy(first_hbm, first, load_sem.at[2]),
        pltpu.make_async_copy(second_hbm, second, load_sem.at[3]),
    ]
    small = [
        pltpu.make_async_copy(source, target, small_sem.at[number])
        for number, (source, target) in enumerate(
            (
                (requests_hbm, requests_ref),
                (slot_hbm, slot_ref),
                (row_hbm, row_ref),
                (col_hbm, col_ref),
                (count_hbm, count_ref),
                (frac_hbm, frac_ref),
                (tvel_hbm, tvel_ref),
            )
        )
    ]
    for load in small + loads[0:2]:
        load.start()
    for load in small:
        load.wait()

    slots = slot_ref[...]
    block = jnp.zeros((DEV, TPP), F32)
    for number in range(4):
        block = jnp.where(slots == number, as_column(requests_ref[number : number + 1, :]), block)
    alive = (lane_index((DEV, TPP)).astype(F32) < as_column(count_ref[...])).astype(F32)
    upper = [block * 8.0 + row_ref[...].astype(F32), col_ref[...].astype(F32), frac_ref[0], frac_ref[1]]
    lower = [tvel_ref[0], tvel_ref[1], tvel_ref[2], alive]
    t_send[:, 0, :] = jnp.concatenate(upper, axis=1)
    t_send[:, 1, :] = jnp.concatenate(lower, axis=1)

    pl.semaphore_wait(barrier, 2 * (DEV - 1))

    def to_holder(step):
        peer = along(gz, step)
        return pltpu.make_async_remote_copy(
            src_ref=t_send.at[peer],
            dst_ref=t_recv.at[gz],
            send_sem=t_ssem.at[step],
            recv_sem=t_rsem.at[step],
            device_id=(gy, peer),
            device_id_type=MESH,
        )

    for step in range(1, DEV):
        to_holder(step).start()
    own = pltpu.make_async_copy(t_send.at[gz], t_recv.at[gz], own_sem.at[0])
    own.start()

    loads[0].wait()
    for comp in range(3):
        for row in range(8):
            cols = slice(comp * 1024 + row * 128, comp * 1024 + (row + 1) * 128)
            vel_b[0:BLOCKS, cols] = widen(vel[comp, pl.ds(row, BLOCKS, stride=8), :]).astype(BF16)
    vel_b[BLOCKS:256, :] = jnp.zeros((256 - BLOCKS, 3072), BF16)
    loads[1].wait()
    for load in loads[2:]:
        load.start()

    @pl.loop(0, PLANES)
    def _(plane):
        rows = pl.ds(pl.multiple_of(plane * LOC, LOC), LOC)
        u = [vel[comp, rows, :] for comp in range(3)]
        w = [vort[comp, rows, :] for comp in range(3)]
        for comp in range(3):
            a, b = (comp + 1) % 3, (comp + 2) % 3
            cross[plane, comp * LOC : (comp + 1) * LOC, :] = widen(u[a] * w[b] - u[b] * w[a])

    own.wait()
    for step in range(1, DEV):
        to_holder(step).wait()

    upper = t_recv[:, 0, :]
    lower = t_recv[:, 1, :]
    turned = jnp.concatenate([upper, lower, jnp.zeros((128 - 2 * DEV, 128), F32)], axis=0).T
    lane_row = lane_index((1, 128))
    for quad in range(4):
        total = jnp.zeros((1, 128), F32)
        for number in range(4):
            owner = quad * 4 + number
            total = jnp.where(
                lane_row // TPP == number, pltpu.roll(upper[owner : owner + 1], number * TPP, 1), total
            )
        row_lanes[0:1, quad * 128 : (quad + 1) * 128] = total

    def field(number, owner):
        rows = slice((number % 4) * TPP, (number % 4 + 1) * TPP)
        col = (number // 4) * DEV + owner
        return jnp.broadcast_to(turned[rows, col : col + 1], (TPP, 128))

    lane = lane_index((TPP, 128))
    lane_f = lane.astype(F32)
    for owner in range(DEV):
        block_at = (field(0, owner).astype(jnp.int32) // 8)
        rows = slice(owner * TPP, (owner + 1) * TPP)
        hot[rows, 0:128] = jnp.where(lane == block_at, 1.0, 0.0).astype(BF16)
        hot[rows, 128:256] = jnp.where(lane + 128 == block_at, 1.0, 0.0).astype(BF16)

    @pl.loop(0, 6)
    def _(tile):
        cols = pl.ds(pl.multiple_of(tile * 512, 512), 512)
        picked[:, cols] = jnp.dot(hot[...], vel_b[:, cols], preferred_element_type=F32)

    back = jnp.zeros((TPP, 128), F32)
    for owner in range(DEV):
        rows = slice(owner * TPP, (owner + 1) * TPP)
        lows = slice(TR + owner * TPP, TR + (owner + 1) * TPP)
        row = jnp.bitwise_and(field(0, owner).astype(jnp.int32), 7)
        start, along_y, along_z = field(1, owner), field(2, owner), field(3, owner)
        cell = jnp.where(lane_f == start, 1.0 - along_z, jnp.where(lane_f == start + 1.0, along_z, 0.0))
        upper_w = (1.0 - along_y) * cell
        lower_w = along_y * cell
        picks = [
            jnp.where(row == number, 1.0 - along_y, jnp.where(row + 1 == number, along_y, 0.0))
            for number in range(8)
        ]
        mass = drag_mass * field(7, owner)
        for comp in range(3):
            line = picks[0] * picked[rows, comp * 1024 : comp * 1024 + 128]
            for number in range(1, 8):
                line += picks[number] * picked[rows, comp * 1024 + number * 128 : comp * 1024 + (number + 1) * 128]
            at = jnp.sum(cell * line, axis=1, keepdims=True)
            back = jnp.where(lane == comp * DEV + owner, at, back)
            drag = mass * (field(4 + comp, owner) - at)
            for weight, place in ((upper_w, rows), (lower_w, lows)):
                value = weight * drag
                high = value.astype(BF16)
                spread[place, comp * 256 : comp * 256 + 128] = high
                spread[place, comp * 256 + 128 : (comp + 1) * 256] = (value - high.astype(F32)).astype(BF16)

    def far(number):
        return jnp.where(number == 0, 2, jnp.where(number == 1, 1, jnp.where(number == 2, 3, 0)))

    def plane_of(step):
        dx, dh = far(lax.rem(step, 4)), far(step // 4)
        return lax.rem(my_x + dx, 4) * 4 + lax.rem(my_h + dh, 4)

    def landing(part):
        return recv1[part].at[pl.ds(0, PIECE[part]), pl.ds(pl.multiple_of(gz * 128, 128), 128)]

    def to_plane(step, part):
        peer = plane_of(step)
        return pltpu.make_async_remote_copy(
            src_ref=send1[part].at[peer],
            dst_ref=landing(part),
            send_sem=sems1[part][0].at[step],
            recv_sem=sems1[part][1].at[step],
            device_id=(gy, peer),
            device_id_type=MESH,
        )

    def own_plane(part):
        return pltpu.make_async_copy(send1[part].at[gz], landing(part), own_sem.at[1 + part])

    starts = row_lanes[0:1, :]

    @pl.loop(0, DEV // 2)
    def _(turn):
        planes = [plane_of(2 * turn), plane_of(2 * turn + 1)]
        hots = []
        for plane in planes:
            cell_row = (lax.broadcasted_iota(jnp.int32, (LOC, TR), 0) + plane * LOC).astype(F32)
            up = jnp.where(cell_row == starts, 1.0, 0.0).astype(BF16)
            down = jnp.where(cell_row == starts + 1.0, 1.0, 0.0).astype(BF16)
            hots.append(jnp.concatenate([up, down], axis=1))
        both = jnp.concatenate(hots, axis=0)
        forces = [[], []]
        for comp in range(3):
            fed = jnp.dot(both, spread[:, comp * 256 : (comp + 1) * 256], preferred_element_type=F32)
            for half in range(2):
                mine = fed[half * LOC : (half + 1) * LOC]
                forces[half].append(
                    cross[planes[half], comp * LOC : (comp + 1) * LOC, :] + (mine[:, 0:128] + mine[:, 128:256])
                )
        for half in range(2):
            for part in range(2):
                low, rows = SPLIT[part]
                main = [
                    forces[half][comp][third * QUARTER + low : third * QUARTER + low + rows]
                    for comp in range(3)
                    for third in range(3)
                ]
                last = [forces[half][comp][72 + low : 72 + low + rows] for comp in range(3)]
                send1[part][planes[half]] = pack(
                    jnp.concatenate(main, axis=0), jnp.concatenate(last, axis=0), part
                ).astype(BF16)
        to_plane(2 * turn, 0).start()

        @pl.when(turn < DEV // 2 - 1)
        def _():
            to_plane(2 * turn + 1, 0).start()

    own_plane(0).start()
    own_plane(1).start()

    done = jnp.concatenate([back, jnp.zeros((128 - TPP, 128), F32)], axis=0).T
    a_send[:, 0, :] = (
        done[0:DEV] + pltpu.roll(done[DEV : 2 * DEV], TPP, 1) + pltpu.roll(done[2 * DEV : 3 * DEV], 2 * TPP, 1)
    )

    def to_owner(step):
        peer = along(gz, step)
        return pltpu.make_async_remote_copy(
            src_ref=a_send.at[peer],
            dst_ref=a_recv.at[gz],
            send_sem=a_ssem.at[step],
            recv_sem=a_rsem.at[step],
            device_id=(gy, peer),
            device_id_type=MESH,
        )

    for step in range(1, DEV):
        to_owner(step).start()
    own_at = pltpu.make_async_copy(a_send.at[gz], a_recv.at[gz], own_sem.at[3])
    own_at.start()

    @pl.loop(0, DEV - 1)
    def _(step):
        to_plane(step, 0).wait_send()

    @pl.loop(0, DEV - 1)
    def _(step):
        to_plane(step, 1).start()

    def chip_of(turn):
        dy = choose(turn, (1, 3, 2, 0, 2, 1, 3, 0))
        dl = choose(turn, (1, 1, 1, 1, 0, 0, 0, 0))
        return lax.rem(gy // 4 + dy, 4) * 2 + lax.rem(gy // 2 + dl, 2)

    def to_waves(step, part):
        peer = chip_of(step // 2) * 2 + lax.rem(gy + step, 2)
        return pltpu.make_async_remote_copy(
            src_ref=send2[part].at[peer],
            dst_ref=recv2[part].at[gy],
            send_sem=sems2[part][0].at[step],
            recv_sem=sems2[part][1].at[step],
            device_id=(peer, gz),
            device_id_type=MESH,
        )

    def own_waves(part):
        return pltpu.make_async_copy(send2[part].at[gy], recv2[part].at[gy], own_sem.at[4 + part])

    def make_pair(turn, part):
        pair = chip_of(turn)
        cols = pl.ds(pl.multiple_of(pair * 256, 256), 256)
        out = jnp.dot(recv1[part][...], first[:, cols], preferred_element_type=F32)
        for half in range(2):
            lanes = slice(half * 128, (half + 1) * 128)
            main = out[0 : MAIN[part], lanes]
            last = out[PIECE[part] : PIECE[part] + LAST[part], lanes]
            send2[part][pair * 2 + half] = pack(main, last, part).astype(BF16)

    def z_transform(part):
        own_plane(part).wait()

        @pl.loop(0, DEV - 1)
        def _(step):
            if part == 1:
                to_plane(step, part).wait_send()
            to_plane(step, part).wait_recv()

        @pl.loop(0, DEV)
        def _(source):
            cols = pl.ds(pl.multiple_of(source * 128, 128), 128)
            piece = recv1[part][0 : PIECE[part], cols].astype(F32)
            recv1[part][PIECE[part] : WIDE[part], cols] = unpack_last(piece, part).astype(BF16)

        @pl.loop(0, 7)
        def _(turn):
            make_pair(turn, part)
            to_waves(2 * turn, part).start()
            to_waves(2 * turn + 1, part).start()

        make_pair(7, part)
        to_waves(15, part).start()
        own_waves(part).start()

    loads[2].wait()
    z_transform(0)
    z_transform(1)

    def y_lines(part):
        own_waves(part).wait()

        @pl.loop(0, DEV - 2)
        def _(step):
            to_waves(step, part).wait()

        to_waves(15, part).wait()

        rows = SPLIT[part][1]
        depth = DEPTH[part] // 2
        quarter = depth // 4
        for comp in range(3):
            re_at, im_at = comp * KZL, (3 + comp) * KZL
            for third in range(3):
                at = (comp * 3 + third) * rows
                stacked = recv2[part][...].astype(F32)[:, at : at + rows].reshape(DEV * rows, 128)
                for piece in range(DEV * rows // 128):
                    tile = stacked[piece * 128 : (piece + 1) * 128].T
                    lo = third * quarter + piece * 128
                    cols, more = slice(lo, lo + 128), slice(depth + lo, depth + lo + 128)
                    real, imag = tile[0:KZL].astype(BF16), tile[KZL : 2 * KZL].astype(BF16)
                    left[part][re_at : re_at + KZL, cols] = real
                    left[part][re_at : re_at + KZL, more] = imag
                    left[part][im_at : im_at + KZL, cols] = imag
                    left[part][im_at : im_at + KZL, more] = -real
                    lo = 3 * quarter + piece * 128
                    cols, more = slice(lo, lo + 128), slice(depth + lo, depth + lo + 128)
                    for half in range(2):
                        value = tile[96 + half * 16 : 112 + half * 16].astype(BF16)
                        kz = third * 32 + half * 16
                        if kz < KZL:
                            left[part][re_at + kz : re_at + kz + 16, cols] = value
                            left[part][im_at + kz : im_at + kz + 16, more] = -value
                        else:
                            kz -= KZL
                            left[part][re_at + kz : re_at + kz + 16, more] = value
                            left[part][im_at + kz : im_at + kz + 16, cols] = value

    loads[3].wait()
    y_lines(0)

    @pl.loop(0, NY // 256)
    def _(tile):
        cols = pl.ds(pl.multiple_of(tile * 256, 256), 256)
        spec[:, cols] = jnp.dot(left_a[...], second[0 : DEPTH[0], cols], preferred_element_type=F32)

    own_at.wait()
    for step in range(1, DEV):
        to_owner(step).wait()
    at_ref[...] = a_recv[:, 0, :]

    y_lines(1)

    def write(tile):
        cols = pl.ds(pl.multiple_of(tile * 256, 256), 256)
        return pltpu.make_async_copy(spec.at[:, cols], spec_hbm.at[:, cols], out_sem.at[tile])

    @pl.loop(0, NY // 256)
    def _(tile):
        cols = pl.ds(pl.multiple_of(tile * 256, 256), 256)
        spec[:, cols] += jnp.dot(left_b[...], second[DEPTH[0] :, cols], preferred_element_type=F32)
        write(tile).start()

    @pl.loop(0, NY // 256)
    def _(tile):
        write(tile).wait()


def update_kernel(
    shift_ref,
    spec_hbm,
    q_hbm,
    u_hbm,
    at_ref,
    count_ref,
    tvel_ref,
    q_out,
    u_out,
    t_out,
    spec,
    q_state,
    u_state,
    in_sem,
    out_sem,
):
    kz_first = lax.axis_index("gy") * KZL
    shift = shift_ref[0]
    tiles_on, lanes_on = shift // 128, lax.rem(shift, 128)
    scale = 1.0 / math.sqrt(NY * NZ)
    lane = lane_index((ROWS, 128))

    def rows_of(ref, chunk):
        return ref.at[:, :, pl.ds(pl.multiple_of(chunk * ROWS, ROWS), ROWS), :]

    def arrive(number, chunk):
        source, target = ((spec_hbm, spec), (q_hbm, q_state), (u_hbm, u_state))[number]
        return pltpu.make_async_copy(rows_of(source, chunk), rows_of(target, chunk), in_sem.at[number, chunk])

    def leave(number, chunk):
        source, target = ((q_state, q_out), (u_state, u_out))[number]
        return pltpu.make_async_copy(rows_of(source, chunk), rows_of(target, chunk), out_sem.at[number, chunk])

    @pl.loop(0, KZL // ROWS)
    def _(chunk):
        for number in range(3):
            arrive(number, chunk).start()

    alive = (lane_index((DEV, TPP)).astype(F32) < as_column(count_ref[...])).astype(F32)
    for comp in range(3):
        old = tvel_ref[comp]
        at = at_ref[:, comp * TPP : (comp + 1) * TPP]
        t_out[comp] = old + relax_ratio * alive * (at - old)

    @pl.loop(0, KZL // ROWS)
    def _(chunk):
        for number in range(3):
            arrive(number, chunk).wait()
        rows = pl.ds(pl.multiple_of(chunk * ROWS, ROWS), ROWS)
        kz = (lax.broadcasted_iota(jnp.int32, (ROWS, 128), 0) + (kz_first + chunk * ROWS)).astype(F32)

        def turned(part, comp, tile):
            at = lax.rem(tile + 24 - tiles_on, 12)
            before = lax.rem(at + 11, 12)
            pieces = [
                spec[part, comp, rows, pl.ds(pl.multiple_of(place * 128, 128), 128)] for place in (before, at)
            ]
            return pltpu.roll(jnp.where(lane >= 128 - lanes_on, pieces[0], pieces[1]), lanes_on, 1)

        for tile in range(NY // 128):
            cols = slice(tile * 128, (tile + 1) * 128)
            kys = (lane + (tile * 128 if tile < 6 else tile * 128 - NY)).astype(F32)
            wave_square = kz * kz + kys * kys
            inverse = 1.0 / jnp.maximum(wave_square, 1.0)
            damping = (time_step * scale) * jnp.exp(-2.0 * wave_square / (NY * NZ))
            for part in range(2):
                moved = [turned(part, comp, tile) for comp in range(3)]
                radial = (kys * moved[1] + kz * moved[2]) * inverse
                projected = [moved[0], moved[1] - kys * radial, moved[2] - kz * radial]
                for comp in range(3):
                    q_new = coef_keep * q_state[part, comp, rows, cols] + damping * projected[comp]
                    q_state[part, comp, rows, cols] = q_new
                    u_state[part, comp, rows, cols] += coef_add * q_new
        for number in range(2):
            leave(number, chunk).start()

    @pl.loop(0, KZL // ROWS)
    def _(chunk):
        for number in range(2):
            leave(number, chunk).wait()


def on_device(
    velocity,
    vorticity,
    q_state,
    u_state,
    shift,
    requests,
    tracer_slot,
    tracer_row,
    tracer_col,
    tracer_count,
    tracer_frac,
    tracer_vel,
):
    first, second = tables()
    hbm = pl.BlockSpec(memory_space=pl.ANY)
    vmem = pl.BlockSpec(memory_space=pltpu.VMEM)
    count = tracer_count.reshape(1, DEV)
    old = tracer_vel.reshape(3, DEV, TPP)
    spectrum, at_tracer = pl.pallas_call(
        exchange_kernel,
        out_shape=(
            jax.ShapeDtypeStruct((6 * KZL, NY), F32),
            jax.ShapeDtypeStruct((DEV, 128), F32),
        ),
        in_specs=[hbm] * 11,
        out_specs=(hbm, vmem),
        scratch_shapes=[
            pltpu.VMEM((4, DEV), jnp.int32),
            pltpu.VMEM((DEV, TPP), jnp.int32),
            pltpu.VMEM((DEV, TPP), jnp.int32),
            pltpu.VMEM((DEV, TPP), jnp.int32),
            pltpu.VMEM((1, DEV), jnp.int32),
            pltpu.VMEM((2, DEV, TPP), F32),
            pltpu.VMEM((3, DEV, TPP), F32),
            pltpu.VMEM((3, CELL_ROWS, LOC), F32),
            pltpu.VMEM((3, CELL_ROWS, LOC), F32),
            pltpu.VMEM((PLANES, 3 * LOC, 128), F32),
            pltpu.VMEM((DEV * 128, DEV * 128), BF16),
            pltpu.VMEM((2 * NY, NY), BF16),
            pltpu.VMEM((256, 3072), BF16),
            pltpu.VMEM((TR, 256), BF16),
            pltpu.VMEM((TR, 3072), F32),
            pltpu.VMEM((2 * TR, 768), BF16),
            pltpu.VMEM((8, TR), F32),
            pltpu.VMEM((DEV, 2, 128), F32),
            pltpu.VMEM((DEV, 2, 128), F32),
            pltpu.VMEM((DEV, 1, 128), F32),
            pltpu.VMEM((DEV, 1, 128), F32),
            pltpu.VMEM((DEV, PIECE[0], 128), BF16),
            pltpu.VMEM((DEV, PIECE[1], 128), BF16),
            pltpu.VMEM((WIDE[0], DEV * 128), BF16),
            pltpu.VMEM((WIDE[1], DEV * 128), BF16),
            pltpu.VMEM((DEV, PIECE[0], 128), BF16),
            pltpu.VMEM((DEV, PIECE[1], 128), BF16),
            pltpu.VMEM((DEV, PIECE[0], 128), BF16),
            pltpu.VMEM((DEV, PIECE[1], 128), BF16),
            pltpu.VMEM((6 * KZL, DEPTH[0]), BF16),
            pltpu.VMEM((6 * KZL, DEPTH[1]), BF16),
            pltpu.VMEM((6 * KZL, NY), F32),
            pltpu.SemaphoreType.DMA((4,)),
            pltpu.SemaphoreType.DMA((7,)),
            pltpu.SemaphoreType.DMA((6,)),
            pltpu.SemaphoreType.DMA((NY // 256,)),
        ]
        + [pltpu.SemaphoreType.DMA((DEV,))] * 12,
        compiler_params=pltpu.CompilerParams(
            collective_id=0, has_side_effects=True, vmem_limit_bytes=56 * 2**20
        ),
        cost_estimate=pl.CostEstimate(flops=6 * 10**9, bytes_accessed=25 * 2**20, transcendentals=0),
        name="exchange",
    )(
        velocity.reshape(3, CELL_ROWS, LOC),
        vorticity.reshape(3, CELL_ROWS, LOC),
        jnp.asarray(first),
        jnp.asarray(second),
        requests.reshape(DEV, 4).T,
        tracer_slot.reshape(DEV, TPP),
        tracer_row.reshape(DEV, TPP),
        tracer_col.reshape(DEV, TPP),
        count,
        tracer_frac.reshape(2, DEV, TPP),
        old,
    )
    q_next, u_next, tracer_next = pl.pallas_call(
        update_kernel,
        out_shape=(
            jax.ShapeDtypeStruct((2, 3, KZL, NY), F32),
            jax.ShapeDtypeStruct((2, 3, KZL, NY), F32),
            jax.ShapeDtypeStruct((3, DEV, TPP), F32),
        ),
        in_specs=[
            pl.BlockSpec(memory_space=pltpu.SMEM),
            hbm,
            hbm,
            hbm,
            vmem,
            vmem,
            vmem,
        ],
        out_specs=(hbm, hbm, vmem),
        scratch_shapes=[
            pltpu.VMEM((2, 3, KZL, NY), F32),
            pltpu.VMEM((2, 3, KZL, NY), F32),
            pltpu.VMEM((2, 3, KZL, NY), F32),
            pltpu.SemaphoreType.DMA((3, KZL // ROWS)),
            pltpu.SemaphoreType.DMA((2, KZL // ROWS)),
        ],
        compiler_params=pltpu.CompilerParams(vmem_limit_bytes=60 * 2**20),
        name="update",
    )(
        shift,
        spectrum.reshape(2, 3, KZL, NY),
        q_state.reshape(2, 3, KZL, NY),
        u_state.reshape(2, 3, KZL, NY),
        at_tracer,
        count,
        old,
    )
    return (
        q_next.reshape(q_state.shape),
        u_next.reshape(u_state.shape),
        tracer_next.reshape(tracer_vel.shape),
    )


def solution(mesh):
    return jax.shard_map(
        on_device,
        mesh=mesh,
        in_specs=(
            P(None, None, "gy", "gz"),
            P(None, None, "gy", "gz"),
            P(None, None, "gz", "gy", None),
            P(None, None, "gz", "gy", None),
            P("gz"),
            P("gy", "gz", None, None),
            P("gy", "gz", None, None),
            P("gy", "gz", None, None),
            P("gy", "gz", None, None),
            P("gy", "gz", None),
            P(None, "gy", "gz", None, None),
            P(None, "gy", "gz", None, None),
        ),
        out_specs=(
            P(None, None, "gz", "gy", None),
            P(None, None, "gz", "gy", None),
            P(None, "gy", "gz", None, None),
        ),
        check_vma=False,
    )
```

```python
import functools
import math

import jax
import jax.numpy as jnp
import ml_dtypes
import numpy as np
from jax import lax
from jax.experimental import pallas as pl
from jax.experimental.pallas import tpu as pltpu
from jax.sharding import PartitionSpec as P

MESH = pl.DeviceIdType.MESH
BF16 = jnp.bfloat16
F32 = jnp.float32

NY = 1536
NZ = 1536
DEV = 16
LOC = 96
PLANES = 16
CELL_ROWS = PLANES * LOC
BLOCKS = 192
KZL = 48
TPP = 32
TR = DEV * TPP
QUARTER = 24
SPLIT = ((0, 16), (16, 8))
MAIN = (144, 72)
PIECE = (144, 80)
LAST = (48, 24)
WIDE = (192, 112)
ROWS = 16
DEPTH = (2048, 1024)

drag_mass = 24.0
relax_ratio = 0.5
coef_keep = -5.0 / 9.0
coef_add = 15.0 / 16.0
time_step = 0.5


def dft_base(length):
    index = np.arange(length, dtype=np.int64)
    phase = (np.outer(index, index) % length).astype(np.float32) * np.float32(2.0 * math.pi / length)
    return np.cos(phase).astype(ml_dtypes.bfloat16), np.sin(phase).astype(ml_dtypes.bfloat16)


@functools.lru_cache(maxsize=None)
def tables():
    cos, sin = dft_base(NY)
    first = np.zeros((DEV, 128, DEV, 128), ml_dtypes.bfloat16)
    kz_cos = cos[:, : NZ // 2].reshape(DEV, LOC, DEV, KZL)
    kz_sin = sin[:, : NZ // 2].reshape(DEV, LOC, DEV, KZL)
    first[:, :LOC, :, :KZL] = kz_cos
    first[:, :LOC, :, KZL : 2 * KZL] = -kz_sin
    second = []
    for low, rows in SPLIT:
        quarter = np.arange(4)[:, None, None]
        source = np.arange(DEV)[None, :, None]
        row = np.arange(rows)[None, None, :]
        row_of = (source * LOC + quarter * QUARTER + low + row).reshape(-1)
        second += [cos[row_of], sin[row_of]]
    return first.reshape(DEV * 128, DEV * 128), np.concatenate(second, axis=0)


def choose(number, values):
    out = values[-1]
    for place in range(len(values) - 2, -1, -1):
        out = jnp.where(number == place, values[place], out)
    return out


def lane_index(shape):
    return lax.broadcasted_iota(jnp.int32, shape, len(shape) - 1)


def pack(main, last, part):
    rows = SPLIT[part][1]
    lane = lane_index((rows, 128))
    out = []
    for comp in range(3):
        low = last[comp * rows : (comp + 1) * rows]
        for third in range(3):
            at = (comp * 3 + third) * rows
            turned = pltpu.roll(low, 96 - 32 * third, 1)
            out.append(jnp.where(lane < LOC, main[at : at + rows], turned))
    if PIECE[part] > MAIN[part]:
        out.append(jnp.zeros((PIECE[part] - MAIN[part], 128), F32))
    return jnp.concatenate(out, axis=0)


def unpack_last(piece, part):
    rows = SPLIT[part][1]
    lane = lane_index((rows, 128))
    out = []
    for comp in range(3):
        parts = [
            pltpu.roll(
                piece[(comp * 3 + third) * rows : (comp * 3 + third + 1) * rows], (32 * third + 32) % 128, 1
            )
            for third in range(3)
        ]
        out.append(
            jnp.where(lane < 32, parts[0], jnp.where(lane < 64, parts[1], jnp.where(lane < LOC, parts[2], 0.0)))
        )
    rest = WIDE[part] - PIECE[part] - LAST[part]
    if rest:
        out.append(jnp.zeros((rest, 128), F32))
    return jnp.concatenate(out, axis=0)


def widen(block):
    return jnp.concatenate([block, jnp.zeros((block.shape[0], 128 - block.shape[1]), block.dtype)], axis=1)


def as_column(row):
    spread = jnp.broadcast_to(row, (DEV, DEV)).astype(F32)
    diagonal = lax.broadcasted_iota(jnp.int32, (DEV, DEV), 0) == lax.broadcasted_iota(jnp.int32, (DEV, DEV), 1)
    return jnp.sum(jnp.where(diagonal, spread, 0.0), axis=1, keepdims=True)


def exchange_kernel(
    vel_hbm,
    vort_hbm,
    first_hbm,
    second_hbm,
    requests_hbm,
    slot_hbm,
    row_hbm,
    col_hbm,
    count_hbm,
    frac_hbm,
    tvel_hbm,
    spec_hbm,
    requests_ref,
    slot_ref,
    row_ref,
    col_ref,
    count_ref,
    frac_ref,
    tvel_ref,
    vel,
    vort,
    cross,
    first,
    second,
    vel_b,
    hot,
    picked,
    spread,
    row_lanes,
    t_send,
    t_recv,
    a_send,
    a_recv,
    send1a,
    send1b,
    recv1a,
    recv1b,
    send2a,
    send2b,
    recv2a,
    recv2b,
    left_a,
    left_b,
    spec,
    load_sem,
    small_sem,
    own_sem,
    out_sem,
    t_ssem,
    t_rsem,
    a_ssem,
    a_rsem,
    ssem1a,
    rsem1a,
    ssem1b,
    rsem1b,
    ssem2a,
    rsem2a,
    ssem2b,
    rsem2b,
):
    gy = lax.axis_index("gy")
    gz = lax.axis_index("gz")
    my_x, my_h = gz // 4, lax.rem(gz, 4)
    send1, recv1 = (send1a, send1b), (recv1a, recv1b)
    send2, recv2 = (send2a, send2b), (recv2a, recv2b)
    sems1 = ((ssem1a, rsem1a), (ssem1b, rsem1b))
    sems2 = ((ssem2a, rsem2a), (ssem2b, rsem2b))
    left = (left_a, left_b)

    def along(base, step):
        return lax.rem(base + step, DEV)

    barrier = pltpu.get_barrier_semaphore()
    for step in range(1, DEV):
        pl.semaphore_signal(barrier, inc=1, device_id=(gy, along(gz, step)), device_id_type=MESH)
    for step in range(1, DEV):
        pl.semaphore_signal(barrier, inc=1, device_id=(along(gy, step), gz), device_id_type=MESH)
    loads = [
        pltpu.make_async_copy(vel_hbm, vel, load_sem.at[0]),
        pltpu.make_async_copy(vort_hbm, vort, load_sem.at[1]),
        pltpu.make_async_copy(first_hbm, first, load_sem.at[2]),
        pltpu.make_async_copy(second_hbm, second, load_sem.at[3]),
    ]
    small = [
        pltpu.make_async_copy(source, target, small_sem.at[number])
        for number, (source, target) in enumerate(
            (
                (requests_hbm, requests_ref),
                (slot_hbm, slot_ref),
                (row_hbm, row_ref),
                (col_hbm, col_ref),
                (count_hbm, count_ref),
                (frac_hbm, frac_ref),
                (tvel_hbm, tvel_ref),
            )
        )
    ]
    for load in small + loads[0:2]:
        load.start()
    for load in small:
        load.wait()

    slots = slot_ref[...]
    block = jnp.zeros((DEV, TPP), F32)
    for number in range(4):
        block = jnp.where(slots == number, as_column(requests_ref[number : number + 1, :]), block)
    alive = (lane_index((DEV, TPP)).astype(F32) < as_column(count_ref[...])).astype(F32)
    upper = [block * 8.0 + row_ref[...].astype(F32), col_ref[...].astype(F32), frac_ref[0], frac_ref[1]]
    lower = [tvel_ref[0], tvel_ref[1], tvel_ref[2], alive]
    t_send[:, 0, :] = jnp.concatenate(upper, axis=1)
    t_send[:, 1, :] = jnp.concatenate(lower, axis=1)

    pl.semaphore_wait(barrier, 2 * (DEV - 1))

    def to_holder(step):
        peer = along(gz, step)
        return pltpu.make_async_remote_copy(
            src_ref=t_send.at[peer],
            dst_ref=t_recv.at[gz],
            send_sem=t_ssem.at[step],
            recv_sem=t_rsem.at[step],
            device_id=(gy, peer),
            device_id_type=MESH,
        )

    for step in range(1, DEV):
        to_holder(step).start()
    own = pltpu.make_async_copy(t_send.at[gz], t_recv.at[gz], own_sem.at[0])
    own.start()

    loads[0].wait()
    for comp in range(3):
        for row in range(8):
            cols = slice(comp * 1024 + row * 128, comp * 1024 + (row + 1) * 128)
            vel_b[0:BLOCKS, cols] = widen(vel[comp, pl.ds(row, BLOCKS, stride=8), :]).astype(BF16)
    vel_b[BLOCKS:256, :] = jnp.zeros((256 - BLOCKS, 3072), BF16)
    loads[1].wait()
    for load in loads[2:]:
        load.start()

    @pl.loop(0, PLANES)
    def _(plane):
        rows = pl.ds(pl.multiple_of(plane * LOC, LOC), LOC)
        u = [vel[comp, rows, :] for comp in range(3)]
        w = [vort[comp, rows, :] for comp in range(3)]
        for comp in range(3):
            a, b = (comp + 1) % 3, (comp + 2) % 3
            cross[plane, comp * LOC : (comp + 1) * LOC, :] = widen(u[a] * w[b] - u[b] * w[a])

    own.wait()
    for step in range(1, DEV):
        to_holder(step).wait()

    upper = t_recv[:, 0, :]
    lower = t_recv[:, 1, :]
    turned = jnp.concatenate([upper, lower, jnp.zeros((128 - 2 * DEV, 128), F32)], axis=0).T
    lane_row = lane_index((1, 128))
    for quad in range(4):
        total = jnp.zeros((1, 128), F32)
        for number in range(4):
            owner = quad * 4 + number
            total = jnp.where(
                lane_row // TPP == number, pltpu.roll(upper[owner : owner + 1], number * TPP, 1), total
            )
        row_lanes[0:1, quad * 128 : (quad + 1) * 128] = total

    def field(number, owner):
        rows = slice((number % 4) * TPP, (number % 4 + 1) * TPP)
        col = (number // 4) * DEV + owner
        return jnp.broadcast_to(turned[rows, col : col + 1], (TPP, 128))

    lane = lane_index((TPP, 128))
    lane_f = lane.astype(F32)
    for owner in range(DEV):
        block_at = (field(0, owner).astype(jnp.int32) // 8)
        rows = slice(owner * TPP, (owner + 1) * TPP)
        hot[rows, 0:128] = jnp.where(lane == block_at, 1.0, 0.0).astype(BF16)
        hot[rows, 128:256] = jnp.where(lane + 128 == block_at, 1.0, 0.0).astype(BF16)

    @pl.loop(0, 6)
    def _(tile):
        cols = pl.ds(pl.multiple_of(tile * 512, 512), 512)
        picked[:, cols] = jnp.dot(hot[...], vel_b[:, cols], preferred_element_type=F32)

    back = jnp.zeros((TPP, 128), F32)
    for owner in range(DEV):
        rows = slice(owner * TPP, (owner + 1) * TPP)
        lows = slice(TR + owner * TPP, TR + (owner + 1) * TPP)
        row = jnp.bitwise_and(field(0, owner).astype(jnp.int32), 7)
        start, along_y, along_z = field(1, owner), field(2, owner), field(3, owner)
        cell = jnp.where(lane_f == start, 1.0 - along_z, jnp.where(lane_f == start + 1.0, along_z, 0.0))
        upper_w = (1.0 - along_y) * cell
        lower_w = along_y * cell
        picks = [
            jnp.where(row == number, 1.0 - along_y, jnp.where(row + 1 == number, along_y, 0.0))
            for number in range(8)
        ]
        mass = drag_mass * field(7, owner)
        for comp in range(3):
            line = picks[0] * picked[rows, comp * 1024 : comp * 1024 + 128]
            for number in range(1, 8):
                line += picks[number] * picked[rows, comp * 1024 + number * 128 : comp * 1024 + (number + 1) * 128]
            at = jnp.sum(cell * line, axis=1, keepdims=True)
            back = jnp.where(lane == comp * DEV + owner, at, back)
            drag = mass * (field(4 + comp, owner) - at)
            for weight, place in ((upper_w, rows), (lower_w, lows)):
                value = weight * drag
                high = value.astype(BF16)
                spread[place, comp * 256 : comp * 256 + 128] = high
                spread[place, comp * 256 + 128 : (comp + 1) * 256] = (value - high.astype(F32)).astype(BF16)

    def far(number):
        return jnp.where(number == 0, 2, jnp.where(number == 1, 1, jnp.where(number == 2, 3, 0)))

    def plane_of(step):
        dx, dh = far(lax.rem(step, 4)), far(step // 4)
        return lax.rem(my_x + dx, 4) * 4 + lax.rem(my_h + dh, 4)

    def landing(part):
        return recv1[part].at[pl.ds(0, PIECE[part]), pl.ds(pl.multiple_of(gz * 128, 128), 128)]

    def to_plane(step, part):
        peer = plane_of(step)
        return pltpu.make_async_remote_copy(
            src_ref=send1[part].at[peer],
            dst_ref=landing(part),
            send_sem=sems1[part][0].at[step],
            recv_sem=sems1[part][1].at[step],
            device_id=(gy, peer),
            device_id_type=MESH,
        )

    def own_plane(part):
        return pltpu.make_async_copy(send1[part].at[gz], landing(part), own_sem.at[1 + part])

    starts = row_lanes[0:1, :]

    @pl.loop(0, DEV // 2)
    def _(turn):
        planes = [plane_of(2 * turn), plane_of(2 * turn + 1)]
        hots = []
        for plane in planes:
            cell_row = (lax.broadcasted_iota(jnp.int32, (LOC, TR), 0) + plane * LOC).astype(F32)
            up = jnp.where(cell_row == starts, 1.0, 0.0).astype(BF16)
            down = jnp.where(cell_row == starts + 1.0, 1.0, 0.0).astype(BF16)
            hots.append(jnp.concatenate([up, down], axis=1))
        both = jnp.concatenate(hots, axis=0)
        forces = [[], []]
        for comp in range(3):
            fed = jnp.dot(both, spread[:, comp * 256 : (comp + 1) * 256], preferred_element_type=F32)
            for half in range(2):
                mine = fed[half * LOC : (half + 1) * LOC]
                forces[half].append(
                    cross[planes[half], comp * LOC : (comp + 1) * LOC, :] + (mine[:, 0:128] + mine[:, 128:256])
                )
        for half in range(2):
            for part in range(2):
                low, rows = SPLIT[part]
                main = [
                    forces[half][comp][third * QUARTER + low : third * QUARTER + low + rows]
                    for comp in range(3)
                    for third in range(3)
                ]
                last = [forces[half][comp][72 + low : 72 + low + rows] for comp in range(3)]
                send1[part][planes[half]] = pack(
                    jnp.concatenate(main, axis=0), jnp.concatenate(last, axis=0), part
                ).astype(BF16)
        to_plane(2 * turn, 0).start()

        @pl.when(turn < DEV // 2 - 1)
        def _():
            to_plane(2 * turn + 1, 0).start()

    own_plane(0).start()
    own_plane(1).start()

    done = jnp.concatenate([back, jnp.zeros((128 - TPP, 128), F32)], axis=0).T
    a_send[:, 0, :] = (
        done[0:DEV] + pltpu.roll(done[DEV : 2 * DEV], TPP, 1) + pltpu.roll(done[2 * DEV : 3 * DEV], 2 * TPP, 1)
    )

    def to_owner(step):
        peer = along(gz, step)
        return pltpu.make_async_remote_copy(
            src_ref=a_send.at[peer],
            dst_ref=a_recv.at[gz],
            send_sem=a_ssem.at[step],
            recv_sem=a_rsem.at[step],
            device_id=(gy, peer),
            device_id_type=MESH,
        )

    for step in range(1, DEV):
        to_owner(step).start()
    own_at = pltpu.make_async_copy(a_send.at[gz], a_recv.at[gz], own_sem.at[3])
    own_at.start()

    @pl.loop(0, DEV - 1)
    def _(step):
        to_plane(step, 0).wait_send()

    @pl.loop(0, DEV - 1)
    def _(step):
        to_plane(step, 1).start()

    def chip_of(turn):
        dy = choose(turn, (1, 3, 2, 0, 2, 1, 3, 0))
        dl = choose(turn, (1, 1, 1, 1, 0, 0, 0, 0))
        return lax.rem(gy // 4 + dy, 4) * 2 + lax.rem(gy // 2 + dl, 2)

    def to_waves(step, part):
        peer = chip_of(step // 2) * 2 + lax.rem(gy + step, 2)
        return pltpu.make_async_remote_copy(
            src_ref=send2[part].at[peer],
            dst_ref=recv2[part].at[gy],
            send_sem=sems2[part][0].at[step],
            recv_sem=sems2[part][1].at[step],
            device_id=(peer, gz),
            device_id_type=MESH,
        )

    def own_waves(part):
        return pltpu.make_async_copy(send2[part].at[gy], recv2[part].at[gy], own_sem.at[4 + part])

    def make_pair(turn, part):
        pair = chip_of(turn)
        cols = pl.ds(pl.multiple_of(pair * 256, 256), 256)
        out = jnp.dot(recv1[part][...], first[:, cols], preferred_element_type=F32)
        for half in range(2):
            lanes = slice(half * 128, (half + 1) * 128)
            main = out[0 : MAIN[part], lanes]
            last = out[PIECE[part] : PIECE[part] + LAST[part], lanes]
            send2[part][pair * 2 + half] = pack(main, last, part).astype(BF16)

    def z_transform(part):
        own_plane(part).wait()

        @pl.loop(0, DEV - 1)
        def _(step):
            if part == 1:
                to_plane(step, part).wait_send()
            to_plane(step, part).wait_recv()

        @pl.loop(0, DEV)
        def _(source):
            cols = pl.ds(pl.multiple_of(source * 128, 128), 128)
            piece = recv1[part][0 : PIECE[part], cols].astype(F32)
            recv1[part][PIECE[part] : WIDE[part], cols] = unpack_last(piece, part).astype(BF16)

        @pl.loop(0, 7)
        def _(turn):
            make_pair(turn, part)
            to_waves(2 * turn, part).start()
            to_waves(2 * turn + 1, part).start()

        make_pair(7, part)
        to_waves(15, part).start()
        own_waves(part).start()

    loads[2].wait()
    z_transform(0)
    z_transform(1)

    def y_lines(part):
        own_waves(part).wait()

        @pl.loop(0, DEV - 2)
        def _(step):
            to_waves(step, part).wait()

        to_waves(15, part).wait()

        rows = SPLIT[part][1]
        depth = DEPTH[part] // 2
        quarter = depth // 4
        for comp in range(3):
            re_at, im_at = comp * KZL, (3 + comp) * KZL
            for third in range(3):
                at = (comp * 3 + third) * rows
                stacked = recv2[part][...].astype(F32)[:, at : at + rows].reshape(DEV * rows, 128)
                for piece in range(DEV * rows // 128):
                    tile = stacked[piece * 128 : (piece + 1) * 128].T
                    lo = third * quarter + piece * 128
                    cols, more = slice(lo, lo + 128), slice(depth + lo, depth + lo + 128)
                    real, imag = tile[0:KZL].astype(BF16), tile[KZL : 2 * KZL].astype(BF16)
                    left[part][re_at : re_at + KZL, cols] = real
                    left[part][re_at : re_at + KZL, more] = imag
                    left[part][im_at : im_at + KZL, cols] = imag
                    left[part][im_at : im_at + KZL, more] = -real
                    lo = 3 * quarter + piece * 128
                    cols, more = slice(lo, lo + 128), slice(depth + lo, depth + lo + 128)
                    for half in range(2):
                        value = tile[96 + half * 16 : 112 + half * 16].astype(BF16)
                        kz = third * 32 + half * 16
                        if kz < KZL:
                            left[part][re_at + kz : re_at + kz + 16, cols] = value
                            left[part][im_at + kz : im_at + kz + 16, more] = -value
                        else:
                            kz -= KZL
                            left[part][re_at + kz : re_at + kz + 16, more] = value
                            left[part][im_at + kz : im_at + kz + 16, cols] = value

    loads[3].wait()
    y_lines(0)

    @pl.loop(0, NY // 256)
    def _(tile):
        cols = pl.ds(pl.multiple_of(tile * 256, 256), 256)
        spec[0 : 6 * KZL, cols] = jnp.dot(left_a[...], second[0 : DEPTH[0], cols], preferred_element_type=F32)

    own_at.wait()
    for step in range(1, DEV):
        to_owner(step).wait()
    spec[6 * KZL :, :] = jnp.zeros((DEV, NY), F32)
    spec[6 * KZL :, 0:128] = a_recv[:, 0, :]

    y_lines(1)

    def write(tile):
        cols = pl.ds(pl.multiple_of(tile * 256, 256), 256)
        return pltpu.make_async_copy(spec.at[:, cols], spec_hbm.at[:, cols], out_sem.at[tile])

    @pl.loop(0, NY // 256)
    def _(tile):
        cols = pl.ds(pl.multiple_of(tile * 256, 256), 256)
        spec[0 : 6 * KZL, cols] += jnp.dot(left_b[...], second[DEPTH[0] :, cols], preferred_element_type=F32)
        write(tile).start()

    @pl.loop(0, NY // 256)
    def _(tile):
        write(tile).wait()


def update_kernel(
    shift_ref,
    spec,
    q_ref,
    u_ref,
    count_ref,
    tvel_ref,
    q_out,
    u_out,
    t_out,
    q_new_ref,
    u_new_ref,
    out_sem,
):
    kz_first = lax.axis_index("gy") * KZL
    shift = shift_ref[0]
    tiles_on, lanes_on = shift // 128, lax.rem(shift, 128)
    scale = 1.0 / math.sqrt(NY * NZ)
    lane = lane_index((ROWS, 128))

    def rows_of(ref, chunk):
        return ref.at[:, :, pl.ds(pl.multiple_of(chunk * ROWS, ROWS), ROWS), :]

    def leave(number, chunk):
        source, target = ((q_new_ref, q_out), (u_new_ref, u_out))[number]
        return pltpu.make_async_copy(rows_of(source, chunk), rows_of(target, chunk), out_sem.at[number, chunk])

    alive = (lane_index((DEV, TPP)).astype(F32) < as_column(count_ref[...])).astype(F32)
    for comp in range(3):
        old = tvel_ref[comp]
        at = spec[6 * KZL :, comp * TPP : (comp + 1) * TPP]
        t_out[comp] = old + relax_ratio * alive * (at - old)

    @pl.loop(0, KZL // ROWS)
    def _(chunk):
        rows = pl.ds(pl.multiple_of(chunk * ROWS, ROWS), ROWS)
        kz = (lax.broadcasted_iota(jnp.int32, (ROWS, 128), 0) + (kz_first + chunk * ROWS)).astype(F32)

        def turned(part, comp, tile):
            at = lax.rem(tile + 24 - tiles_on, 12)
            before = lax.rem(at + 11, 12)
            lines = pl.ds(pl.multiple_of((part * 3 + comp) * KZL + chunk * ROWS, ROWS), ROWS)
            pieces = [spec[lines, pl.ds(pl.multiple_of(place * 128, 128), 128)] for place in (before, at)]
            return pltpu.roll(jnp.where(lane >= 128 - lanes_on, pieces[0], pieces[1]), lanes_on, 1)

        for tile in range(NY // 128):
            cols = slice(tile * 128, (tile + 1) * 128)
            kys = (lane + (tile * 128 if tile < 6 else tile * 128 - NY)).astype(F32)
            wave_square = kz * kz + kys * kys
            inverse = 1.0 / jnp.maximum(wave_square, 1.0)
            damping = (time_step * scale) * jnp.exp(-2.0 * wave_square / (NY * NZ))
            for part in range(2):
                moved = [turned(part, comp, tile) for comp in range(3)]
                radial = (kys * moved[1] + kz * moved[2]) * inverse
                projected = [moved[0], moved[1] - kys * radial, moved[2] - kz * radial]
                for comp in range(3):
                    q_new = coef_keep * q_ref[part, comp, rows, cols] + damping * projected[comp]
                    q_new_ref[part, comp, rows, cols] = q_new
                    u_new_ref[part, comp, rows, cols] = u_ref[part, comp, rows, cols] + coef_add * q_new
        for number in range(2):
            leave(number, chunk).start()

    @pl.loop(0, KZL // ROWS)
    def _(chunk):
        for number in range(2):
            leave(number, chunk).wait()


def on_device(
    velocity,
    vorticity,
    q_state,
    u_state,
    shift,
    requests,
    tracer_slot,
    tracer_row,
    tracer_col,
    tracer_count,
    tracer_frac,
    tracer_vel,
):
    first, second = tables()
    hbm = pl.BlockSpec(memory_space=pl.ANY)
    vmem = pl.BlockSpec(memory_space=pltpu.VMEM)
    count = tracer_count.reshape(1, DEV)
    old = tracer_vel.reshape(3, DEV, TPP)
    spectrum = pl.pallas_call(
        exchange_kernel,
        out_shape=jax.ShapeDtypeStruct((6 * KZL + DEV, NY), F32),
        in_specs=[hbm] * 11,
        out_specs=hbm,
        scratch_shapes=[
            pltpu.VMEM((4, DEV), jnp.int32),
            pltpu.VMEM((DEV, TPP), jnp.int32),
            pltpu.VMEM((DEV, TPP), jnp.int32),
            pltpu.VMEM((DEV, TPP), jnp.int32),
            pltpu.VMEM((1, DEV), jnp.int32),
            pltpu.VMEM((2, DEV, TPP), F32),
            pltpu.VMEM((3, DEV, TPP), F32),
            pltpu.VMEM((3, CELL_ROWS, LOC), F32),
            pltpu.VMEM((3, CELL_ROWS, LOC), F32),
            pltpu.VMEM((PLANES, 3 * LOC, 128), F32),
            pltpu.VMEM((DEV * 128, DEV * 128), BF16),
            pltpu.VMEM((2 * NY, NY), BF16),
            pltpu.VMEM((256, 3072), BF16),
            pltpu.VMEM((TR, 256), BF16),
            pltpu.VMEM((TR, 3072), F32),
            pltpu.VMEM((2 * TR, 768), BF16),
            pltpu.VMEM((8, TR), F32),
            pltpu.VMEM((DEV, 2, 128), F32),
            pltpu.VMEM((DEV, 2, 128), F32),
            pltpu.VMEM((DEV, 1, 128), F32),
            pltpu.VMEM((DEV, 1, 128), F32),
            pltpu.VMEM((DEV, PIECE[0], 128), BF16),
            pltpu.VMEM((DEV, PIECE[1], 128), BF16),
            pltpu.VMEM((WIDE[0], DEV * 128), BF16),
            pltpu.VMEM((WIDE[1], DEV * 128), BF16),
            pltpu.VMEM((DEV, PIECE[0], 128), BF16),
            pltpu.VMEM((DEV, PIECE[1], 128), BF16),
            pltpu.VMEM((DEV, PIECE[0], 128), BF16),
            pltpu.VMEM((DEV, PIECE[1], 128), BF16),
            pltpu.VMEM((6 * KZL, DEPTH[0]), BF16),
            pltpu.VMEM((6 * KZL, DEPTH[1]), BF16),
            pltpu.VMEM((6 * KZL + DEV, NY), F32),
            pltpu.SemaphoreType.DMA((4,)),
            pltpu.SemaphoreType.DMA((7,)),
            pltpu.SemaphoreType.DMA((6,)),
            pltpu.SemaphoreType.DMA((NY // 256,)),
        ]
        + [pltpu.SemaphoreType.DMA((DEV,))] * 12,
        compiler_params=pltpu.CompilerParams(
            collective_id=0, has_side_effects=True, vmem_limit_bytes=56 * 2**20
        ),
        cost_estimate=pl.CostEstimate(flops=6 * 10**9, bytes_accessed=25 * 2**20, transcendentals=0),
        name="exchange",
    )(
        velocity.reshape(3, CELL_ROWS, LOC),
        vorticity.reshape(3, CELL_ROWS, LOC),
        jnp.asarray(first),
        jnp.asarray(second),
        requests.reshape(DEV, 4).T,
        tracer_slot.reshape(DEV, TPP),
        tracer_row.reshape(DEV, TPP),
        tracer_col.reshape(DEV, TPP),
        count,
        tracer_frac.reshape(2, DEV, TPP),
        old,
    )
    q_next, u_next, tracer_next = pl.pallas_call(
        update_kernel,
        out_shape=(
            jax.ShapeDtypeStruct((2, 3, KZL, NY), F32),
            jax.ShapeDtypeStruct((2, 3, KZL, NY), F32),
            jax.ShapeDtypeStruct((3, DEV, TPP), F32),
        ),
        in_specs=[
            pl.BlockSpec(memory_space=pltpu.SMEM),
            vmem,
            vmem,
            vmem,
            vmem,
            vmem,
        ],
        out_specs=(hbm, hbm, vmem),
        scratch_shapes=[
            pltpu.VMEM((2, 3, KZL, NY), F32),
            pltpu.VMEM((2, 3, KZL, NY), F32),
            pltpu.SemaphoreType.DMA((2, KZL // ROWS)),
        ],
        compiler_params=pltpu.CompilerParams(vmem_limit_bytes=32 * 2**20),
        name="update",
    )(
        shift,
        spectrum,
        q_state.reshape(2, 3, KZL, NY),
        u_state.reshape(2, 3, KZL, NY),
        count,
        old,
    )
    return (
        q_next.reshape(q_state.shape),
        u_next.reshape(u_state.shape),
        tracer_next.reshape(tracer_vel.shape),
    )


def solution(mesh):
    return jax.shard_map(
        on_device,
        mesh=mesh,
        in_specs=(
            P(None, None, "gy", "gz"),
            P(None, None, "gy", "gz"),
            P(None, None, "gz", "gy", None),
            P(None, None, "gz", "gy", None),
            P("gz"),
            P("gy", "gz", None, None),
            P("gy", "gz", None, None),
            P("gy", "gz", None, None),
            P("gy", "gz", None, None),
            P("gy", "gz", None),
            P(None, "gy", "gz", None, None),
            P(None, "gy", "gz", None, None),
        ),
        out_specs=(
            P(None, None, "gz", "gy", None),
            P(None, None, "gz", "gy", None),
            P(None, "gy", "gz", None, None),
        ),
        check_vma=False,
    )
```

```python
import functools
import math

import jax
import jax.numpy as jnp
import ml_dtypes
import numpy as np
from jax import lax
from jax.experimental import pallas as pl
from jax.experimental.pallas import tpu as pltpu
from jax.sharding import PartitionSpec as P

MESH = pl.DeviceIdType.MESH
BF16 = jnp.bfloat16
F32 = jnp.float32

NY = 1536
NZ = 1536
DEV = 16
LOC = 96
PLANES = 16
CELL_ROWS = PLANES * LOC
BLOCKS = 192
KZL = 48
TPP = 32
TR = DEV * TPP
QUARTER = 24
SPLIT = ((0, 16), (16, 8))
MAIN = (144, 72)
PIECE = (144, 80)
LAST = (48, 24)
WIDE = (192, 112)
ROWS = 16
DEPTH = (2048, 1024)

drag_mass = 24.0
relax_ratio = 0.5
coef_keep = -5.0 / 9.0
coef_add = 15.0 / 16.0
time_step = 0.5


def dft_base(length):
    index = np.arange(length, dtype=np.int64)
    phase = (np.outer(index, index) % length).astype(np.float32) * np.float32(2.0 * math.pi / length)
    return np.cos(phase).astype(ml_dtypes.bfloat16), np.sin(phase).astype(ml_dtypes.bfloat16)


@functools.lru_cache(maxsize=None)
def tables():
    cos, sin = dft_base(NY)
    first = np.zeros((DEV, 128, DEV, 128), ml_dtypes.bfloat16)
    kz_cos = cos[:, : NZ // 2].reshape(DEV, LOC, DEV, KZL)
    kz_sin = sin[:, : NZ // 2].reshape(DEV, LOC, DEV, KZL)
    first[:, :LOC, :, :KZL] = kz_cos
    first[:, :LOC, :, KZL : 2 * KZL] = -kz_sin
    second = []
    for low, rows in SPLIT:
        quarter = np.arange(4)[:, None, None]
        source = np.arange(DEV)[None, :, None]
        row = np.arange(rows)[None, None, :]
        row_of = (source * LOC + quarter * QUARTER + low + row).reshape(-1)
        second += [cos[row_of], sin[row_of]]
    return first.reshape(DEV * 128, DEV * 128), np.concatenate(second, axis=0)


def choose(number, values):
    out = values[-1]
    for place in range(len(values) - 2, -1, -1):
        out = jnp.where(number == place, values[place], out)
    return out


def lane_index(shape):
    return lax.broadcasted_iota(jnp.int32, shape, len(shape) - 1)


def pack(main, last, part):
    rows = SPLIT[part][1]
    lane = lane_index((rows, 128))
    out = []
    for comp in range(3):
        low = last[comp * rows : (comp + 1) * rows]
        for third in range(3):
            at = (comp * 3 + third) * rows
            turned = pltpu.roll(low, 96 - 32 * third, 1)
            out.append(jnp.where(lane < LOC, main[at : at + rows], turned))
    if PIECE[part] > MAIN[part]:
        out.append(jnp.zeros((PIECE[part] - MAIN[part], 128), F32))
    return jnp.concatenate(out, axis=0)


def unpack_last(piece, part):
    rows = SPLIT[part][1]
    lane = lane_index((rows, 128))
    out = []
    for comp in range(3):
        parts = [
            pltpu.roll(
                piece[(comp * 3 + third) * rows : (comp * 3 + third + 1) * rows], (32 * third + 32) % 128, 1
            )
            for third in range(3)
        ]
        out.append(
            jnp.where(lane < 32, parts[0], jnp.where(lane < 64, parts[1], jnp.where(lane < LOC, parts[2], 0.0)))
        )
    rest = WIDE[part] - PIECE[part] - LAST[part]
    if rest:
        out.append(jnp.zeros((rest, 128), F32))
    return jnp.concatenate(out, axis=0)


def widen(block):
    return jnp.concatenate([block, jnp.zeros((block.shape[0], 128 - block.shape[1]), block.dtype)], axis=1)


def as_column(row):
    spread = jnp.broadcast_to(row, (DEV, DEV)).astype(F32)
    diagonal = lax.broadcasted_iota(jnp.int32, (DEV, DEV), 0) == lax.broadcasted_iota(jnp.int32, (DEV, DEV), 1)
    return jnp.sum(jnp.where(diagonal, spread, 0.0), axis=1, keepdims=True)


def exchange_kernel(
    vel_hbm,
    vort_hbm,
    first_hbm,
    second_hbm,
    requests_hbm,
    slot_hbm,
    row_hbm,
    col_hbm,
    count_hbm,
    frac_hbm,
    tvel_hbm,
    spec_hbm,
    requests_ref,
    slot_ref,
    row_ref,
    col_ref,
    count_ref,
    frac_ref,
    tvel_ref,
    vel,
    vort,
    cross,
    first,
    second,
    vel_b,
    hot,
    picked,
    spread,
    row_lanes,
    t_send,
    t_recv,
    a_send,
    a_recv,
    send1a,
    send1b,
    recv1a,
    recv1b,
    send2a,
    send2b,
    recv2a,
    recv2b,
    left_a,
    left_b,
    spec,
    load_sem,
    small_sem,
    own_sem,
    out_sem,
    t_ssem,
    t_rsem,
    a_ssem,
    a_rsem,
    ssem1a,
    rsem1a,
    ssem1b,
    rsem1b,
    ssem2a,
    rsem2a,
    ssem2b,
    rsem2b,
):
    gy = lax.axis_index("gy")
    gz = lax.axis_index("gz")
    my_x, my_h = gz // 4, lax.rem(gz, 4)
    send1, recv1 = (send1a, send1b), (recv1a, recv1b)
    send2, recv2 = (send2a, send2b), (recv2a, recv2b)
    sems1 = ((ssem1a, rsem1a), (ssem1b, rsem1b))
    sems2 = ((ssem2a, rsem2a), (ssem2b, rsem2b))
    left = (left_a, left_b)

    def along(base, step):
        return lax.rem(base + step, DEV)

    barrier = pltpu.get_barrier_semaphore()
    for step in range(1, DEV):
        pl.semaphore_signal(barrier, inc=1, device_id=(gy, along(gz, step)), device_id_type=MESH)
    for step in range(1, DEV):
        pl.semaphore_signal(barrier, inc=1, device_id=(along(gy, step), gz), device_id_type=MESH)
    loads = [
        pltpu.make_async_copy(vel_hbm, vel, load_sem.at[0]),
        pltpu.make_async_copy(vort_hbm, vort, load_sem.at[1]),
        pltpu.make_async_copy(first_hbm, first, load_sem.at[2]),
        pltpu.make_async_copy(second_hbm, second, load_sem.at[3]),
    ]
    small = [
        pltpu.make_async_copy(source, target, small_sem.at[number])
        for number, (source, target) in enumerate(
            (
                (requests_hbm, requests_ref),
                (slot_hbm, slot_ref),
                (row_hbm, row_ref),
                (col_hbm, col_ref),
                (count_hbm, count_ref),
                (frac_hbm, frac_ref),
                (tvel_hbm, tvel_ref),
            )
        )
    ]
    for load in small + loads[0:2]:
        load.start()
    for load in small:
        load.wait()

    slots = slot_ref[...]
    block = jnp.zeros((DEV, TPP), F32)
    for number in range(4):
        block = jnp.where(slots == number, as_column(requests_ref[number : number + 1, :]), block)
    alive = (lane_index((DEV, TPP)).astype(F32) < as_column(count_ref[...])).astype(F32)
    upper = [block * 8.0 + row_ref[...].astype(F32), col_ref[...].astype(F32), frac_ref[0], frac_ref[1]]
    lower = [tvel_ref[0], tvel_ref[1], tvel_ref[2], alive]
    t_send[:, 0, :] = jnp.concatenate(upper, axis=1)
    t_send[:, 1, :] = jnp.concatenate(lower, axis=1)

    pl.semaphore_wait(barrier, 2 * (DEV - 1))

    def to_holder(step):
        peer = along(gz, step)
        return pltpu.make_async_remote_copy(
            src_ref=t_send.at[peer],
            dst_ref=t_recv.at[gz],
            send_sem=t_ssem.at[step],
            recv_sem=t_rsem.at[step],
            device_id=(gy, peer),
            device_id_type=MESH,
        )

    for step in range(1, DEV):
        to_holder(step).start()
    own = pltpu.make_async_copy(t_send.at[gz], t_recv.at[gz], own_sem.at[0])
    own.start()

    loads[0].wait()
    for comp in range(3):
        for row in range(8):
            cols = slice(comp * 1024 + row * 128, comp * 1024 + (row + 1) * 128)
            vel_b[0:BLOCKS, cols] = widen(vel[comp, pl.ds(row, BLOCKS, stride=8), :]).astype(BF16)
    vel_b[BLOCKS:256, :] = jnp.zeros((256 - BLOCKS, 3072), BF16)
    loads[1].wait()
    for load in loads[2:]:
        load.start()

    @pl.loop(0, PLANES)
    def _(plane):
        rows = pl.ds(pl.multiple_of(plane * LOC, LOC), LOC)
        u = [vel[comp, rows, :] for comp in range(3)]
        w = [vort[comp, rows, :] for comp in range(3)]
        for comp in range(3):
            a, b = (comp + 1) % 3, (comp + 2) % 3
            cross[plane, comp * LOC : (comp + 1) * LOC, :] = widen(u[a] * w[b] - u[b] * w[a])

    own.wait()
    for step in range(1, DEV):
        to_holder(step).wait()

    upper = t_recv[:, 0, :]
    lower = t_recv[:, 1, :]
    turned = jnp.concatenate([upper, lower, jnp.zeros((128 - 2 * DEV, 128), F32)], axis=0).T
    lane_row = lane_index((1, 128))
    for quad in range(4):
        total = jnp.zeros((1, 128), F32)
        for number in range(4):
            owner = quad * 4 + number
            total = jnp.where(
                lane_row // TPP == number, pltpu.roll(upper[owner : owner + 1], number * TPP, 1), total
            )
        row_lanes[0:1, quad * 128 : (quad + 1) * 128] = total

    def field(number, owner):
        rows = slice((number % 4) * TPP, (number % 4 + 1) * TPP)
        col = (number // 4) * DEV + owner
        return jnp.broadcast_to(turned[rows, col : col + 1], (TPP, 128))

    lane = lane_index((TPP, 128))
    lane_f = lane.astype(F32)
    for owner in range(DEV):
        block_at = (field(0, owner).astype(jnp.int32) // 8)
        rows = slice(owner * TPP, (owner + 1) * TPP)
        hot[rows, 0:128] = jnp.where(lane == block_at, 1.0, 0.0).astype(BF16)
        hot[rows, 128:256] = jnp.where(lane + 128 == block_at, 1.0, 0.0).astype(BF16)

    @pl.loop(0, 6)
    def _(tile):
        cols = pl.ds(pl.multiple_of(tile * 512, 512), 512)
        picked[:, cols] = jnp.dot(hot[...], vel_b[:, cols], preferred_element_type=F32)

    back = jnp.zeros((TPP, 128), F32)
    for owner in range(DEV):
        rows = slice(owner * TPP, (owner + 1) * TPP)
        lows = slice(TR + owner * TPP, TR + (owner + 1) * TPP)
        row = jnp.bitwise_and(field(0, owner).astype(jnp.int32), 7)
        start, along_y, along_z = field(1, owner), field(2, owner), field(3, owner)
        cell = jnp.where(lane_f == start, 1.0 - along_z, jnp.where(lane_f == start + 1.0, along_z, 0.0))
        upper_w = (1.0 - along_y) * cell
        lower_w = along_y * cell
        picks = [
            jnp.where(row == number, 1.0 - along_y, jnp.where(row + 1 == number, along_y, 0.0))
            for number in range(8)
        ]
        mass = drag_mass * field(7, owner)
        for comp in range(3):
            line = picks[0] * picked[rows, comp * 1024 : comp * 1024 + 128]
            for number in range(1, 8):
                line += picks[number] * picked[rows, comp * 1024 + number * 128 : comp * 1024 + (number + 1) * 128]
            at = jnp.sum(cell * line, axis=1, keepdims=True)
            back = jnp.where(lane == comp * DEV + owner, at, back)
            drag = mass * (field(4 + comp, owner) - at)
            for weight, place in ((upper_w, rows), (lower_w, lows)):
                value = weight * drag
                high = value.astype(BF16)
                spread[place, comp * 256 : comp * 256 + 128] = high
                spread[place, comp * 256 + 128 : (comp + 1) * 256] = (value - high.astype(F32)).astype(BF16)

    def plane_of(step):
        dx = choose(step, (2, 1, 2, 2, 3, 0, 1, 1, 3, 3, 0, 0, 2, 1, 3, 0))
        dh = choose(step, (2, 2, 1, 3, 2, 2, 1, 3, 1, 3, 1, 3, 0, 0, 0, 0))
        return lax.rem(my_x + dx, 4) * 4 + lax.rem(my_h + dh, 4)

    def landing(part):
        return recv1[part].at[pl.ds(0, PIECE[part]), pl.ds(pl.multiple_of(gz * 128, 128), 128)]

    def to_plane(step, part):
        peer = plane_of(step)
        return pltpu.make_async_remote_copy(
            src_ref=send1[part].at[peer],
            dst_ref=landing(part),
            send_sem=sems1[part][0].at[step],
            recv_sem=sems1[part][1].at[step],
            device_id=(gy, peer),
            device_id_type=MESH,
        )

    def own_plane(part):
        return pltpu.make_async_copy(send1[part].at[gz], landing(part), own_sem.at[1 + part])

    starts = row_lanes[0:1, :]

    @pl.loop(0, DEV // 2)
    def _(turn):
        planes = [plane_of(2 * turn), plane_of(2 * turn + 1)]
        hots = []
        for plane in planes:
            cell_row = (lax.broadcasted_iota(jnp.int32, (LOC, TR), 0) + plane * LOC).astype(F32)
            up = jnp.where(cell_row == starts, 1.0, 0.0).astype(BF16)
            down = jnp.where(cell_row == starts + 1.0, 1.0, 0.0).astype(BF16)
            hots.append(jnp.concatenate([up, down], axis=1))
        both = jnp.concatenate(hots, axis=0)
        forces = [[], []]
        for comp in range(3):
            fed = jnp.dot(both, spread[:, comp * 256 : (comp + 1) * 256], preferred_element_type=F32)
            for half in range(2):
                mine = fed[half * LOC : (half + 1) * LOC]
                forces[half].append(
                    cross[planes[half], comp * LOC : (comp + 1) * LOC, :] + (mine[:, 0:128] + mine[:, 128:256])
                )
        for half in range(2):
            for part in range(2):
                low, rows = SPLIT[part]
                main = [
                    forces[half][comp][third * QUARTER + low : third * QUARTER + low + rows]
                    for comp in range(3)
                    for third in range(3)
                ]
                last = [forces[half][comp][72 + low : 72 + low + rows] for comp in range(3)]
                send1[part][planes[half]] = pack(
                    jnp.concatenate(main, axis=0), jnp.concatenate(last, axis=0), part
                ).astype(BF16)
        to_plane(2 * turn, 0).start()

        @pl.when(turn < DEV // 2 - 1)
        def _():
            to_plane(2 * turn + 1, 0).start()

    own_plane(0).start()
    own_plane(1).start()

    done = jnp.concatenate([back, jnp.zeros((128 - TPP, 128), F32)], axis=0).T
    a_send[:, 0, :] = (
        done[0:DEV] + pltpu.roll(done[DEV : 2 * DEV], TPP, 1) + pltpu.roll(done[2 * DEV : 3 * DEV], 2 * TPP, 1)
    )

    def to_owner(step):
        peer = along(gz, step)
        return pltpu.make_async_remote_copy(
            src_ref=a_send.at[peer],
            dst_ref=a_recv.at[gz],
            send_sem=a_ssem.at[step],
            recv_sem=a_rsem.at[step],
            device_id=(gy, peer),
            device_id_type=MESH,
        )

    for step in range(1, DEV):
        to_owner(step).start()
    own_at = pltpu.make_async_copy(a_send.at[gz], a_recv.at[gz], own_sem.at[3])
    own_at.start()

    @pl.loop(0, DEV - 1)
    def _(step):
        to_plane(step, 0).wait_send()

    @pl.loop(0, DEV - 1)
    def _(step):
        to_plane(step, 1).start()

    def chip_of(turn):
        dy = choose(turn, (1, 3, 2, 0, 2, 1, 3, 0))
        dl = choose(turn, (1, 1, 1, 1, 0, 0, 0, 0))
        return lax.rem(gy // 4 + dy, 4) * 2 + lax.rem(gy // 2 + dl, 2)

    def to_waves(step, part):
        peer = chip_of(step // 2) * 2 + lax.rem(gy + step, 2)
        return pltpu.make_async_remote_copy(
            src_ref=send2[part].at[peer],
            dst_ref=recv2[part].at[gy],
            send_sem=sems2[part][0].at[step],
            recv_sem=sems2[part][1].at[step],
            device_id=(peer, gz),
            device_id_type=MESH,
        )

    def own_waves(part):
        return pltpu.make_async_copy(send2[part].at[gy], recv2[part].at[gy], own_sem.at[4 + part])

    def make_pair(turn, part):
        pair = chip_of(turn)
        cols = pl.ds(pl.multiple_of(pair * 256, 256), 256)
        out = jnp.dot(recv1[part][...], first[:, cols], preferred_element_type=F32)
        for half in range(2):
            lanes = slice(half * 128, (half + 1) * 128)
            main = out[0 : MAIN[part], lanes]
            last = out[PIECE[part] : PIECE[part] + LAST[part], lanes]
            send2[part][pair * 2 + half] = pack(main, last, part).astype(BF16)

    def z_transform(part):
        own_plane(part).wait()

        @pl.loop(0, DEV - 1)
        def _(step):
            if part == 1:
                to_plane(step, part).wait_send()
            to_plane(step, part).wait_recv()

        @pl.loop(0, DEV)
        def _(source):
            cols = pl.ds(pl.multiple_of(source * 128, 128), 128)
            piece = recv1[part][0 : PIECE[part], cols].astype(F32)
            recv1[part][PIECE[part] : WIDE[part], cols] = unpack_last(piece, part).astype(BF16)

        @pl.loop(0, 7)
        def _(turn):
            make_pair(turn, part)
            to_waves(2 * turn, part).start()
            to_waves(2 * turn + 1, part).start()

        make_pair(7, part)
        to_waves(15, part).start()
        own_waves(part).start()

    loads[2].wait()
    z_transform(0)
    z_transform(1)

    def y_lines(part):
        own_waves(part).wait()

        @pl.loop(0, DEV - 2)
        def _(step):
            to_waves(step, part).wait()

        to_waves(15, part).wait()

        rows = SPLIT[part][1]
        depth = DEPTH[part] // 2
        quarter = depth // 4
        for comp in range(3):
            re_at, im_at = comp * KZL, (3 + comp) * KZL
            for third in range(3):
                at = (comp * 3 + third) * rows
                stacked = recv2[part][...].astype(F32)[:, at : at + rows].reshape(DEV * rows, 128)
                for piece in range(DEV * rows // 128):
                    tile = stacked[piece * 128 : (piece + 1) * 128].T
                    lo = third * quarter + piece * 128
                    cols, more = slice(lo, lo + 128), slice(depth + lo, depth + lo + 128)
                    real, imag = tile[0:KZL].astype(BF16), tile[KZL : 2 * KZL].astype(BF16)
                    left[part][re_at : re_at + KZL, cols] = real
                    left[part][re_at : re_at + KZL, more] = imag
                    left[part][im_at : im_at + KZL, cols] = imag
                    left[part][im_at : im_at + KZL, more] = -real
                    lo = 3 * quarter + piece * 128
                    cols, more = slice(lo, lo + 128), slice(depth + lo, depth + lo + 128)
                    for half in range(2):
                        value = tile[96 + half * 16 : 112 + half * 16].astype(BF16)
                        kz = third * 32 + half * 16
                        if kz < KZL:
                            left[part][re_at + kz : re_at + kz + 16, cols] = value
                            left[part][im_at + kz : im_at + kz + 16, more] = -value
                        else:
                            kz -= KZL
                            left[part][re_at + kz : re_at + kz + 16, more] = value
                            left[part][im_at + kz : im_at + kz + 16, cols] = value

    loads[3].wait()
    y_lines(0)

    @pl.loop(0, NY // 256)
    def _(tile):
        cols = pl.ds(pl.multiple_of(tile * 256, 256), 256)
        spec[0 : 6 * KZL, cols] = jnp.dot(left_a[...], second[0 : DEPTH[0], cols], preferred_element_type=F32)

    own_at.wait()
    for step in range(1, DEV):
        to_owner(step).wait()
    spec[6 * KZL :, :] = jnp.zeros((DEV, NY), F32)
    spec[6 * KZL :, 0:128] = a_recv[:, 0, :]

    y_lines(1)

    def write(tile):
        cols = pl.ds(pl.multiple_of(tile * 256, 256), 256)
        return pltpu.make_async_copy(spec.at[:, cols], spec_hbm.at[:, cols], out_sem.at[tile])

    @pl.loop(0, NY // 256)
    def _(tile):
        cols = pl.ds(pl.multiple_of(tile * 256, 256), 256)
        spec[0 : 6 * KZL, cols] += jnp.dot(left_b[...], second[DEPTH[0] :, cols], preferred_element_type=F32)
        write(tile).start()

    @pl.loop(0, NY // 256)
    def _(tile):
        write(tile).wait()


def update_kernel(
    shift_ref,
    spec,
    q_ref,
    u_ref,
    count_ref,
    tvel_ref,
    q_out,
    u_out,
    t_out,
    q_new_ref,
    u_new_ref,
    out_sem,
):
    kz_first = lax.axis_index("gy") * KZL
    shift = shift_ref[0]
    tiles_on, lanes_on = shift // 128, lax.rem(shift, 128)
    scale = 1.0 / math.sqrt(NY * NZ)
    lane = lane_index((ROWS, 128))

    def rows_of(ref, chunk):
        return ref.at[:, :, pl.ds(pl.multiple_of(chunk * ROWS, ROWS), ROWS), :]

    def leave(number, chunk):
        source, target = ((q_new_ref, q_out), (u_new_ref, u_out))[number]
        return pltpu.make_async_copy(rows_of(source, chunk), rows_of(target, chunk), out_sem.at[number, chunk])

    alive = (lane_index((DEV, TPP)).astype(F32) < as_column(count_ref[...])).astype(F32)
    for comp in range(3):
        old = tvel_ref[comp]
        at = spec[6 * KZL :, comp * TPP : (comp + 1) * TPP]
        t_out[comp] = old + relax_ratio * alive * (at - old)

    @pl.loop(0, KZL // ROWS)
    def _(chunk):
        rows = pl.ds(pl.multiple_of(chunk * ROWS, ROWS), ROWS)
        kz = (lax.broadcasted_iota(jnp.int32, (ROWS, 128), 0) + (kz_first + chunk * ROWS)).astype(F32)

        def turned(part, comp, tile):
            at = lax.rem(tile + 24 - tiles_on, 12)
            before = lax.rem(at + 11, 12)
            lines = pl.ds(pl.multiple_of((part * 3 + comp) * KZL + chunk * ROWS, ROWS), ROWS)
            pieces = [spec[lines, pl.ds(pl.multiple_of(place * 128, 128), 128)] for place in (before, at)]
            return pltpu.roll(jnp.where(lane >= 128 - lanes_on, pieces[0], pieces[1]), lanes_on, 1)

        for tile in range(NY // 128):
            cols = slice(tile * 128, (tile + 1) * 128)
            kys = (lane + (tile * 128 if tile < 6 else tile * 128 - NY)).astype(F32)
            wave_square = kz * kz + kys * kys
            inverse = 1.0 / jnp.maximum(wave_square, 1.0)
            damping = (time_step * scale) * jnp.exp(-2.0 * wave_square / (NY * NZ))
            for part in range(2):
                moved = [turned(part, comp, tile) for comp in range(3)]
                radial = (kys * moved[1] + kz * moved[2]) * inverse
                projected = [moved[0], moved[1] - kys * radial, moved[2] - kz * radial]
                for comp in range(3):
                    q_new = coef_keep * q_ref[part, comp, rows, cols] + damping * projected[comp]
                    q_new_ref[part, comp, rows, cols] = q_new
                    u_new_ref[part, comp, rows, cols] = u_ref[part, comp, rows, cols] + coef_add * q_new
        for number in range(2):
            leave(number, chunk).start()

    @pl.loop(0, KZL // ROWS)
    def _(chunk):
        for number in range(2):
            leave(number, chunk).wait()


def on_device(
    velocity,
    vorticity,
    q_state,
    u_state,
    shift,
    requests,
    tracer_slot,
    tracer_row,
    tracer_col,
    tracer_count,
    tracer_frac,
    tracer_vel,
):
    first, second = tables()
    hbm = pl.BlockSpec(memory_space=pl.ANY)
    vmem = pl.BlockSpec(memory_space=pltpu.VMEM)
    count = tracer_count.reshape(1, DEV)
    old = tracer_vel.reshape(3, DEV, TPP)
    spectrum = pl.pallas_call(
        exchange_kernel,
        out_shape=jax.ShapeDtypeStruct((6 * KZL + DEV, NY), F32),
        in_specs=[hbm] * 11,
        out_specs=hbm,
        scratch_shapes=[
            pltpu.VMEM((4, DEV), jnp.int32),
            pltpu.VMEM((DEV, TPP), jnp.int32),
            pltpu.VMEM((DEV, TPP), jnp.int32),
            pltpu.VMEM((DEV, TPP), jnp.int32),
            pltpu.VMEM((1, DEV), jnp.int32),
            pltpu.VMEM((2, DEV, TPP), F32),
            pltpu.VMEM((3, DEV, TPP), F32),
            pltpu.VMEM((3, CELL_ROWS, LOC), F32),
            pltpu.VMEM((3, CELL_ROWS, LOC), F32),
            pltpu.VMEM((PLANES, 3 * LOC, 128), F32),
            pltpu.VMEM((DEV * 128, DEV * 128), BF16),
            pltpu.VMEM((2 * NY, NY), BF16),
            pltpu.VMEM((256, 3072), BF16),
            pltpu.VMEM((TR, 256), BF16),
            pltpu.VMEM((TR, 3072), F32),
            pltpu.VMEM((2 * TR, 768), BF16),
            pltpu.VMEM((8, TR), F32),
            pltpu.VMEM((DEV, 2, 128), F32),
            pltpu.VMEM((DEV, 2, 128), F32),
            pltpu.VMEM((DEV, 1, 128), F32),
            pltpu.VMEM((DEV, 1, 128), F32),
            pltpu.VMEM((DEV, PIECE[0], 128), BF16),
            pltpu.VMEM((DEV, PIECE[1], 128), BF16),
            pltpu.VMEM((WIDE[0], DEV * 128), BF16),
            pltpu.VMEM((WIDE[1], DEV * 128), BF16),
            pltpu.VMEM((DEV, PIECE[0], 128), BF16),
            pltpu.VMEM((DEV, PIECE[1], 128), BF16),
            pltpu.VMEM((DEV, PIECE[0], 128), BF16),
            pltpu.VMEM((DEV, PIECE[1], 128), BF16),
            pltpu.VMEM((6 * KZL, DEPTH[0]), BF16),
            pltpu.VMEM((6 * KZL, DEPTH[1]), BF16),
            pltpu.VMEM((6 * KZL + DEV, NY), F32),
            pltpu.SemaphoreType.DMA((4,)),
            pltpu.SemaphoreType.DMA((7,)),
            pltpu.SemaphoreType.DMA((6,)),
            pltpu.SemaphoreType.DMA((NY // 256,)),
        ]
        + [pltpu.SemaphoreType.DMA((DEV,))] * 12,
        compiler_params=pltpu.CompilerParams(
            collective_id=0, has_side_effects=True, vmem_limit_bytes=56 * 2**20
        ),
        cost_estimate=pl.CostEstimate(flops=6 * 10**9, bytes_accessed=25 * 2**20, transcendentals=0),
        name="exchange",
    )(
        velocity.reshape(3, CELL_ROWS, LOC),
        vorticity.reshape(3, CELL_ROWS, LOC),
        jnp.asarray(first),
        jnp.asarray(second),
        requests.reshape(DEV, 4).T,
        tracer_slot.reshape(DEV, TPP),
        tracer_row.reshape(DEV, TPP),
        tracer_col.reshape(DEV, TPP),
        count,
        tracer_frac.reshape(2, DEV, TPP),
        old,
    )
    q_next, u_next, tracer_next = pl.pallas_call(
        update_kernel,
        out_shape=(
            jax.ShapeDtypeStruct((2, 3, KZL, NY), F32),
            jax.ShapeDtypeStruct((2, 3, KZL, NY), F32),
            jax.ShapeDtypeStruct((3, DEV, TPP), F32),
        ),
        in_specs=[
            pl.BlockSpec(memory_space=pltpu.SMEM),
            vmem,
            vmem,
            vmem,
            vmem,
            vmem,
        ],
        out_specs=(hbm, hbm, vmem),
        scratch_shapes=[
            pltpu.VMEM((2, 3, KZL, NY), F32),
            pltpu.VMEM((2, 3, KZL, NY), F32),
            pltpu.SemaphoreType.DMA((2, KZL // ROWS)),
        ],
        compiler_params=pltpu.CompilerParams(vmem_limit_bytes=32 * 2**20),
        name="update",
    )(
        shift,
        spectrum,
        q_state.reshape(2, 3, KZL, NY),
        u_state.reshape(2, 3, KZL, NY),
        count,
        old,
    )
    return (
        q_next.reshape(q_state.shape),
        u_next.reshape(u_state.shape),
        tracer_next.reshape(tracer_vel.shape),
    )


def solution(mesh):
    return jax.shard_map(
        on_device,
        mesh=mesh,
        in_specs=(
            P(None, None, "gy", "gz"),
            P(None, None, "gy", "gz"),
            P(None, None, "gz", "gy", None),
            P(None, None, "gz", "gy", None),
            P("gz"),
            P("gy", "gz", None, None),
            P("gy", "gz", None, None),
            P("gy", "gz", None, None),
            P("gy", "gz", None, None),
            P("gy", "gz", None),
            P(None, "gy", "gz", None, None),
            P(None, "gy", "gz", None, None),
        ),
        out_specs=(
            P(None, None, "gz", "gy", None),
            P(None, None, "gz", "gy", None),
            P(None, "gy", "gz", None, None),
        ),
        check_vma=False,
    )
```
